128 devices in a mesh: pa: 32 (over x, z, core), mu: 4 (over y).
Axes of the slice: x: 4, y: 4, z: 4, core: 2. Of those that a mesh axis runs over, the one named last changes fastest.
Arguments:
- tensor: bfloat16 [1536, 512, 512], P('pa'), may hold values from -6 to 6
- block_mask: int32 [24, 8, 8], replicated, may hold values from 0 to 1, as said below
- group_of_block: int32 [8], replicated, may hold values from 0 to 3, never falling along the last dimension, each value on 1 to 3 neighbouring positions
- green_occ: bfloat16 [512, 512], replicated, may hold values from -0.25 to 0.25
- green_virt: bfloat16 [512, 512], replicated, may hold values from -0.25 to 0.25
Outputs:
- chi: float32 [1536, 1536], P('pa', 'mu')
The draws below stay inside these ranges and needn't reach their ends.
Inputs may be any that keep to these rules, and one draw needn't show every extreme that they name: `block_mask`: entries are 0 or 1; the share of ones differs from one RI block to another. `group_of_block`: group numbers never fall along the AO blocks; each group holds 1 to 3 blocks.
All inputs are finite; a program needn't handle non-finite values.
Results may differ from the reference program's by a relative error of at most 0.004.
Values may be sent and summed in bfloat16 or wider, within the bound.
A program may use at most 192 MiB of HBM per device.

```python
import math
import jax
import jax.numpy as jnp
import numpy as np
from jax import lax

BS = 64
NAB = 8
GROUP_REACH = 1
NAO = 512
NP = 1536
NPB = 24
NGROUP = 4


def draw_block_mask(key, part):
    key = jax.random.fold_in(key, 11)
    level_key, roll_key = jax.random.split(key)
    level = jax.random.randint(level_key, (NPB, 1, 1), 1, 9)
    roll = jax.random.randint(roll_key, (NPB, NAB, NAB), 0, 16)
    return (roll < level).astype(jnp.int32)


def steps_of(stream_key, shape, pieces, smallest, top_value):
    factor_of = 1.0
    for dim, blocks in pieces:
        steps = jax.random.uniform(jax.random.fold_in(jax.random.fold_in(stream_key, 6), dim), (blocks,), jnp.float32, smallest / len(pieces), top_value / len(pieces))
        factor_of = factor_of * jnp.repeat(jnp.exp(steps), shape[dim] // blocks).reshape((-1,) + (1,) * (len(shape) - 1 - dim))
    return factor_of


def profile(number_of, total, limit, skew):
    weights = [(1 << 20) // math.isqrt(rank ** skew) + 1 for rank in range(2, number_of + 1)]
    rest, counts = total - limit - (number_of - 1), [1] * (number_of - 1)
    while rest > 0:
        free = [i for i in range(number_of - 1) if counts[i] < limit]
        whole, left = sum([weights[i] for i in free]), rest
        for i in free:
            more = min(limit - counts[i], max(1, left * weights[i] // whole), rest)
            counts[i] = counts[i] + more
            rest = rest - more
    return np.array([limit] + counts)


def ragged_sizes(key, number_of, total, reach, lean):
    if number_of == 2:
        one = jax.random.randint(key, (), max(1, total - reach), min(reach, total - 1) + 1)
        return jnp.stack([one, total - one])
    sizes = jnp.asarray(profile(number_of, total, reach, lean), jnp.int32)
    couples = (number_of - 1) // 2
    donor, receiver = sizes[1:1 + 2 * couples:2], sizes[2:2 + 2 * couples:2]
    slack = jnp.minimum(donor - 1, reach - receiver)
    passed = jax.random.randint(jax.random.fold_in(key, 1), (couples,), 0, 1 << 20) % (slack + 1)
    sizes = sizes.at[1:1 + 2 * couples:2].set(donor - passed).at[2:2 + 2 * couples:2].set(receiver + passed)
    return sizes[jax.random.permutation(jax.random.fold_in(key, 2), number_of)]


def noise(key, extent, scale, reach, shards=(), kind=jnp.bfloat16):
    values = jax.random.normal(key, extent, jnp.float32) * scale
    if len(shards) > 0:
        values = steps_of(key, extent, shards, -0.22, 0.18) * values
    return jnp.clip(values, min=-reach, max=reach).astype(kind)


def setup_inputs(seed: int = 0) -> dict:
    keys = jax.random.split(jax.random.key(seed), 6)
    tensor = noise(keys[0], (NP, NAO, NAO), 1.0, 6.0, ((0, 32),))
    block_mask = draw_block_mask(jax.random.fold_in(keys[5], 71), 0)
    group_of_block = jnp.searchsorted(jnp.cumsum(ragged_sizes(keys[2], NGROUP, NAB, 3, 0)), jnp.arange(NAB), side="right").astype(jnp.int32)
    green_occ = noise(keys[3], (NAO, NAO), NAO ** -0.5, 0.25)
    green_virt = noise(keys[4], (NAO, NAO), NAO ** -0.5, 0.25)
    return {"tensor": tensor, "block_mask": block_mask, "group_of_block": group_of_block, "green_occ": green_occ, "green_virt": green_virt}


def reference(tensor, block_mask, group_of_block, green_occ, green_virt):
    rows_mask = jnp.repeat(block_mask, BS, axis=0)
    expanded = jnp.repeat(rows_mask, BS, axis=2).astype(tensor.dtype)
    masked = (tensor.reshape(NP, NAB, BS, NAO) * expanded[:, :, None, :]).reshape(NP, NAO, NAO)
    groups = jnp.repeat(group_of_block, BS)
    keep = (jnp.abs(groups[:, None] - groups[None, :]) <= GROUP_REACH).astype(green_occ.dtype)
    occ = (green_occ * keep).astype(jnp.float32)
    virt = (green_virt * keep).astype(jnp.float32)

    def transform(block):
        half = jnp.einsum('ml,pmn->pln', occ, block.astype(jnp.float32)).astype(jnp.bfloat16)
        return jnp.einsum('pln,ns->pls', half.astype(jnp.float32), virt).astype(jnp.bfloat16)

    product = lax.map(transform, masked.reshape(NP // BS, BS, NAO, NAO)).reshape(NP, NAO * NAO)
    chi = jnp.dot(product, masked.reshape(NP, NAO * NAO).T, preferred_element_type=jnp.float32)
    return chi * (1.0 / NAO)
```

```python
import jax
import jax.numpy as jnp
from jax import lax
from jax.experimental import pallas as pl
from jax.experimental.pallas import tpu as pltpu
from jax.sharding import PartitionSpec as P

MESH = pl.DeviceIdType.MESH
F32, BF16 = jnp.float32, jnp.bfloat16

BS = 64
GROUP_REACH = 1
NX = NZ = NY = 4
CHIPS = NX * NZ
ROWS = 48
NP = 1536
NAO = 512
LB = 16
SB = 128
KC = LB * SB
XW = 3
XR = ROWS // XW
YW = 6
YR = ROWS // YW
WR = CHIPS * YR
QC = NP // NY
NEAR = [(1, 0), (0, 1), (-1, 0), (0, -1), (1, 1), (-1, -1), (1, -1), (-1, 1), (2, 0), (0, 2), (2, 1), (1, 2), (2, -1), (-1, 2), (2, 2)]
DY = (2, 1, 3)


def block_of(shape, dim, first=0):
    return lax.broadcasted_iota(jnp.int32, shape, dim) // BS + first


def kernel(
    tensor, mask, group, occ, virt, out,
    xr, xl, tb, me, occ_t, vm, mv, perm, half, ys, yr, yl, cb, sb, yrs, zr,
    x_send, x_recv, l_send, l_recv, t_sem, y_send, y_recv, c_send, c_recv, z_send, z_recv,
):
    pa, mu = lax.axis_index("pa"), lax.axis_index("mu")
    x, z, core = pa // (2 * NZ), lax.rem(pa // 2, NZ), lax.rem(pa, 2)
    chip = x * NZ + z

    def moved(dx, dz):
        return lax.rem(x + dx + NX, NX), lax.rem(z + dz + NZ, NZ)

    def plane(x2, z2, c2):
        return ((x2 * NZ + z2) * 2 + c2, mu)

    def tensor_chunk(w):
        return pltpu.make_async_copy(tensor.at[pl.ds(w * YR, YR)], tb.at[lax.rem(w, 2)], t_sem.at[lax.rem(w, 2)])

    tensor_chunk(0).start()
    barrier = pltpu.get_barrier_semaphore()
    for c2 in (0, 1):
        for dx, dz in NEAR + [(0, 0)]:
            if (dx, dz, c2) != (0, 0, 0):
                pl.semaphore_signal(barrier, inc=1, device_id=plane(*moved(dx, dz), lax.rem(core + c2, 2)), device_id_type=MESH)
    for dy in DY:
        pl.semaphore_signal(barrier, inc=1, device_id=(pa, lax.rem(mu + dy, NY)), device_id_type=MESH)
    pl.semaphore_wait(barrier, 2 * CHIPS - 1 + NY - 1)

    def send_x(w, carry):
        def part(x2, z2, c2):
            return tensor.at[
                pl.ds(w * XR, XR),
                pl.ds(pl.multiple_of(mu * (NAO // NY) + x2 * 2 * LB + c2 * LB, LB), LB),
                pl.ds(pl.multiple_of(z2 * SB, SB), SB),
            ]

        for c2 in (0, 1):
            for dx, dz in NEAR + [(0, 0)]:
                where = (*moved(dx, dz), lax.rem(core + c2, 2))
                if (dx, dz, c2) == (0, 0, 0):
                    pltpu.make_async_copy(part(*where), xr.at[w, pa], x_recv.at[w]).start()
                else:
                    pltpu.make_async_remote_copy(
                        src_ref=part(*where), dst_ref=xr.at[w, pa], send_sem=x_send.at[w], recv_sem=x_recv.at[w],
                        device_id=plane(*where), device_id_type=MESH,
                    ).start()
        return carry

    lax.fori_loop(0, XW, send_x, 0)

    spread = (block_of((NAO, 8), 0) == lax.broadcasted_iota(jnp.int32, (NAO, 8), 1)).astype(F32)
    for g in range(3):
        blocks = mask[(ROWS * pa + 16 * g) // BS].astype(F32)
        rows = jnp.dot(spread, blocks, preferred_element_type=F32)
        me[g] = lax.dot_general(rows, spread, (((1,), (1,)), ((), ())), preferred_element_type=F32).astype(BF16)
    lane_block = lax.broadcasted_iota(jnp.int32, (8, SB), 0) == block_of((8, SB), 1, 2 * z)
    own_blocks = mask[:, pl.ds(2 * mu + x // 2, 1), :].astype(F32).reshape(NP // BS, 8)
    mv[...] = jnp.dot(own_blocks, lane_block.astype(F32), preferred_element_type=F32)
    group_row = group[...].astype(F32)
    row_group = jnp.sum(spread * group_row, axis=1, keepdims=True)
    col_group = lax.dot_general(group_row, spread, (((1,), (1,)), ((), ())), preferred_element_type=F32)
    vm[...] = jnp.where(jnp.abs(row_group - col_group) <= GROUP_REACH + 0.5, virt[...].astype(F32), 0.0).astype(BF16)
    occ_block = lax.broadcasted_iota(jnp.int32, (8, SB), 0) == block_of((8, SB), 1, 2 * mu)
    occ_group = jnp.dot(group_row, occ_block.astype(F32), preferred_element_type=F32)
    occ_cols = occ[:, pl.ds(pl.multiple_of(mu * SB, SB), SB)].astype(F32)
    occ_cols = jnp.where(jnp.abs(row_group - occ_group) <= GROUP_REACH + 0.5, occ_cols, 0.0)
    occ_t[...] = occ_cols.T.astype(BF16)
    to = lax.broadcasted_iota(jnp.int32, (256, 256), 0)
    perm[...] = (lax.broadcasted_iota(jnp.int32, (256, 256), 1) == lax.rem(to, 16) * 16 + to // 16).astype(BF16)

    def send_y(w):
        def part(x2, z2):
            return ys.at[pl.ds(w * YR, YR), pl.ds(pl.multiple_of(x2 * 2 * LB, 2 * LB), 2 * LB), pl.ds(pl.multiple_of(z2 * SB, SB), SB)]

        for dx, dz in NEAR:
            x2, z2 = moved(dx, dz)
            pltpu.make_async_remote_copy(
                src_ref=part(x2, z2), dst_ref=yr.at[w, chip], send_sem=y_send.at[w], recv_sem=y_recv.at[w],
                device_id=plane(x2, z2, core), device_id_type=MESH,
            ).start()
        pltpu.make_async_copy(part(x, z), yr.at[w, chip], y_recv.at[w]).start()

    def make_product(w, carry):
        tensor_chunk(w).wait()

        @pl.when(w + 1 < YW)
        def _():
            tensor_chunk(w + 1).start()

        slot = lax.rem(w, 2)

        def one(p, carry):
            block = tb[slot, p] * me[w // 2]
            half[pl.ds(pl.multiple_of(p * SB, SB), SB), :] = jnp.dot(occ_t[...], block, preferred_element_type=F32).astype(BF16)
            return carry

        lax.fori_loop(0, YR, one, 0)

        def two(i, carry):
            rows = half[pl.ds(pl.multiple_of(i * 2 * SB, 2 * SB), 2 * SB), :]
            done = jnp.dot(rows, vm[...], preferred_element_type=F32).astype(BF16)
            ys[pl.ds(w * YR + 2 * i, 2)] = done.reshape(2, SB, NAO)
            return carry

        lax.fori_loop(0, YR // 2, two, 0)
        send_y(w)
        return carry

    lax.fori_loop(0, YW, make_product, 0)

    def sibling(rows, columns):
        return pltpu.make_async_remote_copy(
            src_ref=xl.at[rows, columns], dst_ref=xl.at[rows, columns], send_sem=l_send, recv_sem=l_recv,
            device_id=plane(x, z, 1 - core), device_id_type=MESH,
        )

    own = pl.multiple_of(core * KC, KC)
    other = pl.multiple_of((1 - core) * KC, KC)

    def turn(rows):
        return jnp.dot(perm[...], rows, preferred_element_type=F32).astype(BF16).reshape(16, 16, SB)

    def lay_x(w, carry):
        pltpu.make_async_copy(xr.at[w], xr.at[w], x_recv.at[w]).wait()

        def one(j, carry):
            row = pl.multiple_of(j * ROWS + w * XR, XR)
            keep = mv[pl.ds(row // BS, 1), :].astype(BF16)
            turned = turn(xr[w, j].reshape(256, SB) * keep)
            for i in range(LB):
                xl[pl.ds(row, XR), pl.ds(pl.multiple_of(own + i * SB, SB), SB)] = turned[i]
            sibling(pl.ds(row, XR), pl.ds(own, KC)).start()
            return carry

        lax.fori_loop(0, 2 * CHIPS, one, 0)
        return carry

    lax.fori_loop(0, XW, lay_x, 0)
    pltpu.make_async_copy(xl.at[:, pl.ds(other, KC)], xl.at[:, pl.ds(other, KC)], l_recv).wait()

    def partial(w, carry):
        pltpu.make_async_copy(yr.at[w], yr.at[w], y_recv.at[w]).wait()

        def lay_y(i, carry):
            for h in (0, 1):
                turned = turn(yr[w, pl.ds(2 * i, 2), :, h * LB : (h + 1) * LB, :].reshape(256, SB))
                for k in range(LB):
                    yl[pl.ds(pl.multiple_of(i * 16, 16), 16), (h * LB + k) * SB : (h * LB + k + 1) * SB] = turned[k]
            return carry

        lax.fori_loop(0, CHIPS // 2, lay_y, 0)

        def tile(y2):
            columns = xl[pl.ds(pl.multiple_of(y2 * QC, QC), QC), :]
            return lax.dot_general(yl[...], columns, (((1,), (1,)), ((), ())), preferred_element_type=F32)

        for k, dy in enumerate(DY):
            y2 = lax.rem(mu + dy, NY)
            cb[w, k] = tile(y2)
            pltpu.make_async_remote_copy(
                src_ref=cb.at[w, k], dst_ref=yrs.at[w, k], send_sem=c_send.at[w], recv_sem=c_recv.at[w],
                device_id=(pa, y2), device_id_type=MESH,
            ).start()
        sb[w] = tile(mu)

        @pl.when(w > 0)
        def _():
            sum_y(w - 1)

        return carry

    def sum_y(w):
        pltpu.make_async_copy(yrs.at[w], yrs.at[w], c_recv.at[w]).wait()
        sb[w] = (sb[w] + yrs[w, 0]) + (yrs[w, 1] + yrs[w, 2])

        def part(there):
            return sb.at[w, pl.ds(pl.multiple_of(there * YR, YR), YR)]

        for dx, dz in NEAR:
            x2, z2 = moved(dx, dz)
            pltpu.make_async_remote_copy(
                src_ref=part(x2 * NZ + z2), dst_ref=zr.at[w, chip], send_sem=z_send.at[w], recv_sem=z_recv.at[w],
                device_id=plane(x2, z2, core), device_id_type=MESH,
            ).start()
        pltpu.make_async_copy(part(chip), zr.at[w, chip], z_recv.at[w]).start()

    lax.fori_loop(0, YW, partial, 0)
    sum_y(YW - 1)

    def finish(w, carry):
        pltpu.make_async_copy(zr.at[w], zr.at[w], z_recv.at[w]).wait()
        out[pl.ds(pl.multiple_of(w * YR, YR), YR), :] = jnp.sum(zr[w], axis=0) * (1.0 / NAO)
        return carry

    lax.fori_loop(0, YW, finish, 0)

    def left(ref, sem):
        pltpu.make_async_copy(ref, ref, sem).wait()

    left(xl.at[:, pl.ds(own, KC)], l_send)
    for w in range(XW):
        left(xr.at[w, pl.ds(0, 2 * CHIPS - 1)], x_send.at[w])
    for w in range(YW):
        left(yr.at[w, pl.ds(0, CHIPS - 1)], y_send.at[w])
        left(cb.at[w], c_send.at[w])
        left(zr.at[w, pl.ds(0, CHIPS - 1)], z_send.at[w])


def shards(tensor, block_mask, group_of_block, green_occ, green_virt):
    vmem = pl.BlockSpec(memory_space=pltpu.VMEM)
    dma = pltpu.SemaphoreType.DMA
    return pl.pallas_call(
        kernel,
        out_shape=jax.ShapeDtypeStruct((ROWS, QC), F32),
        in_specs=[pl.BlockSpec(memory_space=pl.ANY), vmem, vmem, vmem, vmem],
        out_specs=vmem,
        scratch_shapes=[
            pltpu.VMEM((XW, 2 * CHIPS, XR, LB, SB), BF16),
            pltpu.VMEM((NP, 2 * KC), BF16),
            pltpu.VMEM((2, YR, NAO, NAO), BF16),
            pltpu.VMEM((3, NAO, NAO), BF16),
            pltpu.VMEM((SB, NAO), BF16),
            pltpu.VMEM((NAO, NAO), BF16),
            pltpu.VMEM((NP // BS, SB), F32),
            pltpu.VMEM((256, 256), BF16),
            pltpu.VMEM((YR * SB, NAO), BF16),
            pltpu.VMEM((ROWS, SB, NAO), BF16),
            pltpu.VMEM((YW, CHIPS, YR, 2 * LB, SB), BF16),
            pltpu.VMEM((WR, 2 * KC), BF16),
            pltpu.VMEM((YW, NY - 1, WR, QC), F32),
            pltpu.VMEM((YW, WR, QC), F32),
            pltpu.VMEM((YW, NY - 1, WR, QC), F32),
            pltpu.VMEM((YW, CHIPS, YR, QC), F32),
            dma((XW,)), dma((XW,)), dma, dma, dma((2,)), dma((YW,)), dma((YW,)), dma((YW,)), dma((YW,)), dma((YW,)), dma((YW,)),
        ],
        compiler_params=pltpu.CompilerParams(collective_id=0, has_side_effects=True, vmem_limit_bytes=60 * 2**20),
    )(tensor, block_mask, group_of_block.reshape(1, 8), green_occ, green_virt)


def solution(mesh):
    placed = (P("pa", None, None), P(), P(), P(), P())
    return jax.shard_map(shards, mesh=mesh, in_specs=placed, out_specs=P("pa", "mu"), check_vma=False)
```

```python
import jax
import jax.numpy as jnp
from jax import lax
from jax.experimental import pallas as pl
from jax.experimental.pallas import tpu as pltpu
from jax.sharding import PartitionSpec as P

MESH = pl.DeviceIdType.MESH
F32, BF16 = jnp.float32, jnp.bfloat16

BS = 64
GROUP_REACH = 1
NX = NZ = NY = 4
CHIPS = NX * NZ
ROWS = 48
NP = 1536
NAO = 512
LB = 16
SB = 128
KC = LB * SB
XW = 3
XR = ROWS // XW
YW = 6
YR = ROWS // YW
TR = 8
ZW = 3
ZR = ROWS // ZW
YZ = ZR // YR
WR = CHIPS * YR
QC = NP // NY
NEAR = [(1, 0), (0, 1), (-1, 0), (0, -1), (1, 1), (-1, -1), (1, -1), (-1, 1), (2, 0), (0, 2), (2, 1), (1, 2), (2, -1), (-1, 2), (2, 2)]
DY = (2, 1, 3)


def block_of(shape, dim, first=0):
    return lax.broadcasted_iota(jnp.int32, shape, dim) // BS + first


def kernel(
    tensor, mask, group, occ, virt, out,
    xr, xl, tb, me, occ_t, vm, mv, perm, half, ys, yr, yl, cb, sb, yrs, zf, zb, zr,
    x_send, x_recv, l_send, l_recv, t_sem, y_send, y_recv, c_send, c_recv, z_send, z_recv,
):
    pa, mu = lax.axis_index("pa"), lax.axis_index("mu")
    x, z, core = pa // (2 * NZ), lax.rem(pa // 2, NZ), lax.rem(pa, 2)
    chip = x * NZ + z

    def moved(dx, dz):
        return lax.rem(x + dx + core * (dz - dx) + NX, NX), lax.rem(z + dz + core * (dx - dz) + NZ, NZ)

    def plane(x2, z2, c2):
        return ((x2 * NZ + z2) * 2 + c2, mu)

    def tensor_chunk(w):
        return pltpu.make_async_copy(tensor.at[pl.ds(w * TR, TR)], tb.at[lax.rem(w, 2)], t_sem.at[lax.rem(w, 2)])

    tensor_chunk(0).start()
    barrier = pltpu.get_barrier_semaphore()
    for c2 in (0, 1):
        for dx, dz in NEAR + [(0, 0)]:
            if (dx, dz, c2) != (0, 0, 0):
                pl.semaphore_signal(barrier, inc=1, device_id=plane(*moved(dx, dz), lax.rem(core + c2, 2)), device_id_type=MESH)
    for dy in DY:
        pl.semaphore_signal(barrier, inc=1, device_id=(pa, lax.rem(mu + dy, NY)), device_id_type=MESH)
    pl.semaphore_wait(barrier, 2 * CHIPS - 1 + NY - 1)

    def send_x(w, carry):
        def part(x2, z2, c2):
            return tensor.at[
                pl.ds(w * XR, XR),
                pl.ds(pl.multiple_of(mu * (NAO // NY) + x2 * 2 * LB + c2 * LB, LB), LB),
                pl.ds(pl.multiple_of(z2 * SB, SB), SB),
            ]

        for c2 in (0, 1):
            for dx, dz in NEAR + [(0, 0)]:
                where = (*moved(dx, dz), lax.rem(core + c2, 2))
                if (dx, dz, c2) == (0, 0, 0):
                    pltpu.make_async_copy(part(*where), xr.at[w, pa], x_recv.at[w]).start()
                else:
                    pltpu.make_async_remote_copy(
                        src_ref=part(*where), dst_ref=xr.at[w, pa], send_sem=x_send.at[w], recv_sem=x_recv.at[w],
                        device_id=plane(*where), device_id_type=MESH,
                    ).start()
        return carry

    lax.fori_loop(0, XW, send_x, 0)

    spread = (block_of((NAO, 8), 0) == lax.broadcasted_iota(jnp.int32, (NAO, 8), 1)).astype(F32)
    for g in range(3):
        blocks = mask[(ROWS * pa + 16 * g) // BS].astype(F32)
        rows = jnp.dot(spread, blocks, preferred_element_type=F32)
        me[g] = lax.dot_general(rows, spread, (((1,), (1,)), ((), ())), preferred_element_type=F32).astype(BF16)
    lane_block = lax.broadcasted_iota(jnp.int32, (8, SB), 0) == block_of((8, SB), 1, 2 * z)
    own_blocks = mask[:, pl.ds(2 * mu + x // 2, 1), :].astype(F32).reshape(NP // BS, 8)
    mv[...] = jnp.dot(own_blocks, lane_block.astype(F32), preferred_element_type=F32)
    group_row = group[...].astype(F32)
    row_group = jnp.sum(spread * group_row, axis=1, keepdims=True)
    col_group = lax.dot_general(group_row, spread, (((1,), (1,)), ((), ())), preferred_element_type=F32)
    vm[...] = jnp.where(jnp.abs(row_group - col_group) <= GROUP_REACH + 0.5, virt[...].astype(F32), 0.0).astype(BF16)
    occ_block = lax.broadcasted_iota(jnp.int32, (8, SB), 0) == block_of((8, SB), 1, 2 * mu)
    occ_group = jnp.dot(group_row, occ_block.astype(F32), preferred_element_type=F32)
    occ_cols = occ[:, pl.ds(pl.multiple_of(mu * SB, SB), SB)].astype(F32)
    occ_cols = jnp.where(jnp.abs(row_group - occ_group) <= GROUP_REACH + 0.5, occ_cols, 0.0)
    occ_t[...] = occ_cols.T.astype(BF16)
    to = lax.broadcasted_iota(jnp.int32, (256, 256), 0)
    perm[...] = (lax.broadcasted_iota(jnp.int32, (256, 256), 1) == lax.rem(to, 16) * 16 + to // 16).astype(BF16)

    def send_y(w):
        def part(x2, z2):
            return ys.at[pl.ds(w * YR, YR), pl.ds(pl.multiple_of(x2 * 2 * LB, 2 * LB), 2 * LB), pl.ds(pl.multiple_of(z2 * SB, SB), SB)]

        for dx, dz in NEAR:
            x2, z2 = moved(dx, dz)
            pltpu.make_async_remote_copy(
                src_ref=part(x2, z2), dst_ref=yr.at[w, chip], send_sem=y_send.at[w], recv_sem=y_recv.at[w],
                device_id=plane(x2, z2, core), device_id_type=MESH,
            ).start()
        pltpu.make_async_copy(part(x, z), yr.at[w, chip], y_recv.at[w]).start()

    def make_product(w, carry):
        tensor_chunk(w).wait()

        @pl.when(w + 1 < ROWS // TR)
        def _():
            tensor_chunk(w + 1).start()

        slot = lax.rem(w, 2)

        def one(p, carry):
            block = tb[slot, p] * me[w // 2]
            half[pl.ds(pl.multiple_of(p * SB, SB), SB), :] = jnp.dot(occ_t[...], block, preferred_element_type=F32).astype(BF16)
            return carry

        lax.fori_loop(0, TR, one, 0)

        def two(i, carry):
            rows = half[pl.ds(pl.multiple_of(i * 2 * SB, 2 * SB), 2 * SB), :]
            done = jnp.dot(rows, vm[...], preferred_element_type=F32).astype(BF16)
            ys[pl.ds(w * TR + 2 * i, 2)] = done.reshape(2, SB, NAO)
            return carry

        lax.fori_loop(0, TR // 2, two, 0)
        for k in range(TR // YR):
            send_y(w * (TR // YR) + k)
        return carry

    lax.fori_loop(0, ROWS // TR, make_product, 0)

    def sibling(rows, columns):
        return pltpu.make_async_remote_copy(
            src_ref=xl.at[rows, columns], dst_ref=xl.at[rows, columns], send_sem=l_send, recv_sem=l_recv,
            device_id=plane(x, z, 1 - core), device_id_type=MESH,
        )

    own = pl.multiple_of(core * KC, KC)
    other = pl.multiple_of((1 - core) * KC, KC)

    def turn(rows):
        return jnp.dot(perm[...], rows, preferred_element_type=F32).astype(BF16).reshape(16, 16, SB)

    def lay_x(w, carry):
        pltpu.make_async_copy(xr.at[w], xr.at[w], x_recv.at[w]).wait()

        def one(j, carry):
            row = pl.multiple_of(j * ROWS + w * XR, XR)
            keep = mv[pl.ds(row // BS, 1), :].astype(BF16)
            turned = turn(xr[w, j].reshape(256, SB) * keep)
            for i in range(LB):
                xl[pl.ds(row, XR), pl.ds(pl.multiple_of(own + i * SB, SB), SB)] = turned[i]
            sibling(pl.ds(row, XR), pl.ds(own, KC)).start()
            return carry

        lax.fori_loop(0, 2 * CHIPS, one, 0)
        return carry

    lax.fori_loop(0, XW, lay_x, 0)
    pltpu.make_async_copy(xl.at[:, pl.ds(other, KC)], xl.at[:, pl.ds(other, KC)], l_recv).wait()

    def partial(w, carry):
        pltpu.make_async_copy(yr.at[w], yr.at[w], y_recv.at[w]).wait()

        def lay_y(i, carry):
            for h in (0, 1):
                turned = turn(yr[w, pl.ds(16 // YR * i, 16 // YR), :, h * LB : (h + 1) * LB, :].reshape(256, SB))
                for k in range(LB):
                    yl[pl.ds(pl.multiple_of(i * 16, 16), 16), (h * LB + k) * SB : (h * LB + k + 1) * SB] = turned[k]
            return carry

        lax.fori_loop(0, WR // 16, lay_y, 0)

        def tile(y2):
            columns = xl[pl.ds(pl.multiple_of(y2 * QC, QC), QC), :]
            return lax.dot_general(yl[...], columns, (((1,), (1,)), ((), ())), preferred_element_type=F32)

        for k, dy in enumerate(DY):
            y2 = lax.rem(mu + dy, NY)
            cb[w, k] = tile(y2).astype(BF16)
            pltpu.make_async_remote_copy(
                src_ref=cb.at[w, k], dst_ref=yrs.at[w, k], send_sem=c_send.at[w], recv_sem=c_recv.at[w],
                device_id=(pa, y2), device_id_type=MESH,
            ).start()
        sb[lax.rem(w, 2)] = tile(mu)

        @pl.when(w > 0)
        def _():
            sum_y(w - 1)

        return carry

    def sum_y(w):
        pltpu.make_async_copy(yrs.at[w], yrs.at[w], c_recv.at[w]).wait()
        total = (sb[lax.rem(w, 2)] + yrs[w, 0].astype(F32)) + (yrs[w, 1].astype(F32) + yrs[w, 2].astype(F32))
        for k in range(YZ):

            @pl.when(lax.rem(w, YZ) == k)
            def _():
                zf[:, k * YR : (k + 1) * YR, :] = total.reshape(CHIPS, YR, QC)

        @pl.when(lax.rem(w, YZ) == YZ - 1)
        def _():
            send_z(w // YZ)

    def send_z(v):
        zb[v] = zf[...].astype(BF16)
        for dx, dz in NEAR:
            x2, z2 = moved(dx, dz)
            pltpu.make_async_remote_copy(
                src_ref=zb.at[v, x2 * NZ + z2], dst_ref=zr.at[v, chip], send_sem=z_send.at[v], recv_sem=z_recv.at[v],
                device_id=plane(x2, z2, core), device_id_type=MESH,
            ).start()
        pltpu.make_async_copy(zb.at[v, chip], zr.at[v, chip], z_recv.at[v]).start()

    lax.fori_loop(0, YW, partial, 0)
    sum_y(YW - 1)

    def finish(w, carry):
        pltpu.make_async_copy(zr.at[w], zr.at[w], z_recv.at[w]).wait()
        out[pl.ds(pl.multiple_of(w * ZR, ZR), ZR), :] = jnp.sum(zr[w].astype(F32), axis=0) * (1.0 / NAO)
        return carry

    lax.fori_loop(0, ZW, finish, 0)

    def left(ref, sem):
        pltpu.make_async_copy(ref, ref, sem).wait()

    left(xl.at[:, pl.ds(own, KC)], l_send)
    for w in range(XW):
        left(xr.at[w, pl.ds(0, 2 * CHIPS - 1)], x_send.at[w])
    for w in range(YW):
        left(yr.at[w, pl.ds(0, CHIPS - 1)], y_send.at[w])
        left(cb.at[w], c_send.at[w])
    for w in range(ZW):
        left(zr.at[w, pl.ds(0, CHIPS - 1)], z_send.at[w])


def shards(tensor, block_mask, group_of_block, green_occ, green_virt):
    vmem = pl.BlockSpec(memory_space=pltpu.VMEM)
    dma = pltpu.SemaphoreType.DMA
    return pl.pallas_call(
        kernel,
        out_shape=jax.ShapeDtypeStruct((ROWS, QC), F32),
        in_specs=[pl.BlockSpec(memory_space=pl.ANY), vmem, vmem, vmem, vmem],
        out_specs=vmem,
        scratch_shapes=[
            pltpu.VMEM((XW, 2 * CHIPS, XR, LB, SB), BF16),
            pltpu.VMEM((NP, 2 * KC), BF16),
            pltpu.VMEM((2, TR, NAO, NAO), BF16),
            pltpu.VMEM((3, NAO, NAO), BF16),
            pltpu.VMEM((SB, NAO), BF16),
            pltpu.VMEM((NAO, NAO), BF16),
            pltpu.VMEM((NP // BS, SB), F32),
            pltpu.VMEM((256, 256), BF16),
            pltpu.VMEM((TR * SB, NAO), BF16),
            pltpu.VMEM((ROWS, SB, NAO), BF16),
            pltpu.VMEM((YW, CHIPS, YR, 2 * LB, SB), BF16),
            pltpu.VMEM((WR, 2 * KC), BF16),
            pltpu.VMEM((YW, NY - 1, WR, QC), BF16),
            pltpu.VMEM((2, WR, QC), F32),
            pltpu.VMEM((YW, NY - 1, WR, QC), BF16),
            pltpu.VMEM((CHIPS, ZR, QC), F32),
            pltpu.VMEM((ZW, CHIPS, ZR, QC), BF16),
            pltpu.VMEM((ZW, CHIPS, ZR, QC), BF16),
            dma((XW,)), dma((XW,)), dma, dma, dma((2,)), dma((YW,)), dma((YW,)), dma((YW,)), dma((YW,)), dma((ZW,)), dma((ZW,)),
        ],
        compiler_params=pltpu.CompilerParams(collective_id=0, has_side_effects=True, vmem_limit_bytes=60 * 2**20),
    )(tensor, block_mask, group_of_block.reshape(1, 8), green_occ, green_virt)


def solution(mesh):
    placed = (P("pa", None, None), P(), P(), P(), P())
    return jax.shard_map(shards, mesh=mesh, in_specs=placed, out_specs=P("pa", "mu"), check_vma=False)
```

```python
import jax
import jax.numpy as jnp
from jax import lax
from jax.experimental import pallas as pl
from jax.experimental.pallas import tpu as pltpu
from jax.sharding import PartitionSpec as P

MESH = pl.DeviceIdType.MESH
F32, BF16 = jnp.float32, jnp.bfloat16

BS = 64
GROUP_REACH = 1
NX = NZ = NY = 4
CHIPS = NX * NZ
ROWS = 48
NP = 1536
NAO = 512
LB = 16
SB = 128
KC = LB * SB
XW = 3
XR = ROWS // XW
YW = 6
YR = ROWS // YW
TR = 8
ZW = 3
ZR = ROWS // ZW
YZ = ZR // YR
WR = CHIPS * YR
QC = NP // NY
NEAR = [(1, 0), (0, 1), (-1, 0), (0, -1), (1, 1), (-1, -1), (1, -1), (-1, 1), (2, 0), (0, 2), (2, 1), (1, 2), (2, -1), (-1, 2), (2, 2)]
DY = (2, 1, 3)


SLOTS = 60
PW = 4
UNITS = 3 * 64
SR = 4


def block_of(shape, dim, first=0):
    return lax.broadcasted_iota(jnp.int32, shape, dim) // BS + first


def kernel(
    tensor, mask, group, occ, virt, out,
    xr, xl, tb, me, occ_t, vm, mv, perm, half, ys, yr, yl, cb, sb, yrs, zf, zb, zr,
    x_send, x_recv, l_send, l_recv, t_sem, y_send, y_recv, c_send, c_recv, z_send, z_recv,
):
    pa, mu = lax.axis_index("pa"), lax.axis_index("mu")
    x, z, core = pa // (2 * NZ), lax.rem(pa // 2, NZ), lax.rem(pa, 2)
    chip = x * NZ + z

    def moved(dx, dz):
        return lax.rem(x + dx + core * (dz - dx) + NX, NX), lax.rem(z + dz + core * (dx - dz) + NZ, NZ)

    def plane(x2, z2, c2):
        return ((x2 * NZ + z2) * 2 + c2, mu)

    def tensor_chunk(w):
        return pltpu.make_async_copy(tensor.at[pl.ds(w * TR, TR)], tb.at[lax.rem(w, 2)], t_sem.at[lax.rem(w, 2)])

    tensor_chunk(0).start()
    barrier = pltpu.get_barrier_semaphore()
    for c2 in (0, 1):
        for dx, dz in NEAR + [(0, 0)]:
            if (dx, dz, c2) != (0, 0, 0):
                pl.semaphore_signal(barrier, inc=1, device_id=plane(*moved(dx, dz), lax.rem(core + c2, 2)), device_id_type=MESH)
    for dy in DY:
        pl.semaphore_signal(barrier, inc=1, device_id=(pa, lax.rem(mu + dy, NY)), device_id_type=MESH)
    pl.semaphore_wait(barrier, 2 * CHIPS - 1 + NY - 1)

    def send_x(w, carry):
        def part(x2, z2, c2):
            return tensor.at[
                pl.ds(w * XR, XR),
                pl.ds(pl.multiple_of(mu * (NAO // NY) + x2 * 2 * LB + c2 * LB, LB), LB),
                pl.ds(pl.multiple_of(z2 * SB, SB), SB),
            ]

        for c2 in (0, 1):
            for dx, dz in NEAR + [(0, 0)]:
                where = (*moved(dx, dz), lax.rem(core + c2, 2))
                if (dx, dz, c2) == (0, 0, 0):
                    pltpu.make_async_copy(part(*where), xr.at[w, pa], x_recv.at[w]).start()
                else:
                    pltpu.make_async_remote_copy(
                        src_ref=part(*where), dst_ref=xr.at[w, pa], send_sem=x_send.at[w], recv_sem=x_recv.at[w],
                        device_id=plane(*where), device_id_type=MESH,
                    ).start()
        return carry

    lax.fori_loop(0, XW, send_x, 0)

    spread = (block_of((NAO, 8), 0) == lax.broadcasted_iota(jnp.int32, (NAO, 8), 1)).astype(F32)
    for g in range(3):
        blocks = mask[(ROWS * pa + 16 * g) // BS].astype(F32)
        rows = jnp.dot(spread, blocks, preferred_element_type=F32)
        me[g] = lax.dot_general(rows, spread, (((1,), (1,)), ((), ())), preferred_element_type=F32).astype(BF16)
    lane_block = lax.broadcasted_iota(jnp.int32, (8, SB), 0) == block_of((8, SB), 1, 2 * z)
    own_blocks = mask[:, pl.ds(2 * mu + x // 2, 1), :].astype(F32).reshape(NP // BS, 8)
    mv[...] = jnp.dot(own_blocks, lane_block.astype(F32), preferred_element_type=F32)
    group_row = group[...].astype(F32)
    row_group = jnp.sum(spread * group_row, axis=1, keepdims=True)
    col_group = lax.dot_general(group_row, spread, (((1,), (1,)), ((), ())), preferred_element_type=F32)
    vm[...] = jnp.where(jnp.abs(row_group - col_group) <= GROUP_REACH + 0.5, virt[...].astype(F32), 0.0).astype(BF16)
    occ_block = lax.broadcasted_iota(jnp.int32, (8, SB), 0) == block_of((8, SB), 1, 2 * mu)
    occ_group = jnp.dot(group_row, occ_block.astype(F32), preferred_element_type=F32)
    occ_cols = occ[:, pl.ds(pl.multiple_of(mu * SB, SB), SB)].astype(F32)
    occ_cols = jnp.where(jnp.abs(row_group - occ_group) <= GROUP_REACH + 0.5, occ_cols, 0.0)
    occ_t[...] = occ_cols.T.astype(BF16)
    to = lax.broadcasted_iota(jnp.int32, (256, 256), 0)
    perm[...] = (lax.broadcasted_iota(jnp.int32, (256, 256), 1) == lax.rem(to, 16) * 16 + to // 16).astype(BF16)

    def send_y(w):
        def part(x2, z2):
            return ys.at[pl.ds(w * YR, YR), pl.ds(pl.multiple_of(x2 * 2 * LB, 2 * LB), 2 * LB), pl.ds(pl.multiple_of(z2 * SB, SB), SB)]

        for dx, dz in NEAR:
            x2, z2 = moved(dx, dz)
            pltpu.make_async_remote_copy(
                src_ref=part(x2, z2), dst_ref=yr.at[w, chip], send_sem=y_send.at[w], recv_sem=y_recv.at[w],
                device_id=plane(x2, z2, core), device_id_type=MESH,
            ).start()
        pltpu.make_async_copy(part(x, z), yr.at[w, chip], y_recv.at[w]).start()

    def make_product(w, carry):
        tensor_chunk(w).wait()

        @pl.when(w + 1 < ROWS // TR)
        def _():
            tensor_chunk(w + 1).start()

        slot = lax.rem(w, 2)

        def one(p, carry):
            block = tb[slot, p] * me[w // 2]
            half[pl.ds(pl.multiple_of(p * SB, SB), SB), :] = jnp.dot(occ_t[...], block, preferred_element_type=F32).astype(BF16)
            return carry

        lax.fori_loop(0, TR, one, 0)

        def two(i, carry):
            rows = half[pl.ds(pl.multiple_of(i * 2 * SB, 2 * SB), 2 * SB), :]
            done = jnp.dot(rows, vm[...], preferred_element_type=F32).astype(BF16)
            ys[pl.ds(w * TR + 2 * i, 2)] = done.reshape(2, SB, NAO)
            return carry

        lax.fori_loop(0, TR // 2, two, 0)
        for k in range(TR // YR):
            send_y(w * (TR // YR) + k)
        return carry

    lax.fori_loop(0, ROWS // TR, make_product, 0)

    def sibling(rows, columns):
        return pltpu.make_async_remote_copy(
            src_ref=xl.at[rows, columns], dst_ref=xl.at[rows, columns], send_sem=l_send, recv_sem=l_recv,
            device_id=plane(x, z, 1 - core), device_id_type=MESH,
        )

    own = pl.multiple_of(core * KC, KC)
    other = pl.multiple_of((1 - core) * KC, KC)

    def turn(rows):
        return jnp.dot(perm[...], rows, preferred_element_type=F32).astype(BF16).reshape(16, 16, SB)

    def lay_x(w, carry):
        pltpu.make_async_copy(xr.at[w], xr.at[w], x_recv.at[w]).wait()

        def one(j, carry):
            row = pl.multiple_of(j * ROWS + w * XR, XR)
            keep = mv[pl.ds(row // BS, 1), :].astype(BF16)
            turned = turn(xr[w, j].reshape(256, SB) * keep)
            for i in range(LB):
                xl[pl.ds(row, XR), pl.ds(pl.multiple_of(own + i * SB, SB), SB)] = turned[i]
            sibling(pl.ds(row, XR), pl.ds(own, KC)).start()
            return carry

        lax.fori_loop(0, 2 * CHIPS, one, 0)
        return carry

    lax.fori_loop(0, XW, lay_x, 0)
    pltpu.make_async_copy(xl.at[:, pl.ds(other, KC)], xl.at[:, pl.ds(other, KC)], l_recv).wait()

    def partial(w, carry):
        pltpu.make_async_copy(yr.at[w], yr.at[w], y_recv.at[w]).wait()

        def lay_y(i, carry):
            for h in (0, 1):
                turned = turn(yr[w, pl.ds(16 // YR * i, 16 // YR), :, h * LB : (h + 1) * LB, :].reshape(256, SB))
                for k in range(LB):
                    yl[pl.ds(pl.multiple_of(i * 16, 16), 16), (h * LB + k) * SB : (h * LB + k + 1) * SB] = turned[k]
            return carry

        lax.fori_loop(0, WR // 16, lay_y, 0)

        def tile(y2):
            columns = xl[pl.ds(pl.multiple_of(y2 * QC, QC), QC), :]
            return lax.dot_general(yl[...], columns, (((1,), (1,)), ((), ())), preferred_element_type=F32)

        for k, dy in enumerate(DY):
            y2 = lax.rem(mu + dy, NY)
            cb[w, k] = tile(y2).astype(BF16)
            pltpu.make_async_remote_copy(
                src_ref=cb.at[w, k], dst_ref=yrs.at[w, k], send_sem=c_send.at[w], recv_sem=c_recv.at[w],
                device_id=(pa, y2), device_id_type=MESH,
            ).start()
        sb[lax.rem(w, 2)] = tile(mu)

        @pl.when(w > 0)
        def _():
            sum_y(w - 1)

        return carry

    def sum_y(w):
        pltpu.make_async_copy(yrs.at[w], yrs.at[w], c_recv.at[w]).wait()
        total = (sb[lax.rem(w, 2)] + yrs[w, 0].astype(F32)) + (yrs[w, 1].astype(F32) + yrs[w, 2].astype(F32))
        for k in range(YZ):

            @pl.when(lax.rem(w, YZ) == k)
            def _():
                zf[:, k * YR : (k + 1) * YR, :] = total.reshape(CHIPS, YR, QC)

        @pl.when(lax.rem(w, YZ) == YZ - 1)
        def _():
            send_z(w // YZ)

    def send_z(v):
        zb[v] = zf[...].astype(BF16)
        for dx, dz in NEAR:
            x2, z2 = moved(dx, dz)
            pltpu.make_async_remote_copy(
                src_ref=zb.at[v, x2 * NZ + z2], dst_ref=zr.at[v, chip], send_sem=z_send.at[v], recv_sem=z_recv.at[v],
                device_id=plane(x2, z2, core), device_id_type=MESH,
            ).start()
        pltpu.make_async_copy(zb.at[v, chip], zr.at[v, chip], z_recv.at[v]).start()

    lax.fori_loop(0, YW, partial, 0)
    sum_y(YW - 1)

    def finish(w, carry):
        pltpu.make_async_copy(zr.at[w], zr.at[w], z_recv.at[w]).wait()
        out[pl.ds(pl.multiple_of(w * ZR, ZR), ZR), :] = jnp.sum(zr[w].astype(F32), axis=0) * (1.0 / NAO)
        return carry

    lax.fori_loop(0, ZW, finish, 0)

    def left(ref, sem):
        pltpu.make_async_copy(ref, ref, sem).wait()

    left(xl.at[:, pl.ds(own, KC)], l_send)
    for w in range(XW):
        left(xr.at[w, pl.ds(0, 2 * CHIPS - 1)], x_send.at[w])
    for w in range(YW):
        left(yr.at[w, pl.ds(0, CHIPS - 1)], y_send.at[w])
        left(cb.at[w], c_send.at[w])
    for w in range(ZW):
        left(zr.at[w, pl.ds(0, CHIPS - 1)], z_send.at[w])


def whole(tensor, block_mask, group_row, green_occ, green_virt):
    vmem = pl.BlockSpec(memory_space=pltpu.VMEM)
    dma = pltpu.SemaphoreType.DMA
    return pl.pallas_call(
        kernel,
        out_shape=jax.ShapeDtypeStruct((ROWS, QC), F32),
        in_specs=[pl.BlockSpec(memory_space=pl.ANY), vmem, vmem, vmem, vmem],
        out_specs=vmem,
        scratch_shapes=[
            pltpu.VMEM((XW, 2 * CHIPS, XR, LB, SB), BF16),
            pltpu.VMEM((NP, 2 * KC), BF16),
            pltpu.VMEM((2, TR, NAO, NAO), BF16),
            pltpu.VMEM((3, NAO, NAO), BF16),
            pltpu.VMEM((SB, NAO), BF16),
            pltpu.VMEM((NAO, NAO), BF16),
            pltpu.VMEM((NP // BS, SB), F32),
            pltpu.VMEM((256, 256), BF16),
            pltpu.VMEM((TR * SB, NAO), BF16),
            pltpu.VMEM((ROWS, SB, NAO), BF16),
            pltpu.VMEM((YW, CHIPS, YR, 2 * LB, SB), BF16),
            pltpu.VMEM((WR, 2 * KC), BF16),
            pltpu.VMEM((YW, NY - 1, WR, QC), BF16),
            pltpu.VMEM((2, WR, QC), F32),
            pltpu.VMEM((YW, NY - 1, WR, QC), BF16),
            pltpu.VMEM((CHIPS, ZR, QC), F32),
            pltpu.VMEM((ZW, CHIPS, ZR, QC), BF16),
            pltpu.VMEM((ZW, CHIPS, ZR, QC), BF16),
            dma((XW,)), dma((XW,)), dma, dma, dma((2,)), dma((YW,)), dma((YW,)), dma((YW,)), dma((YW,)), dma((ZW,)), dma((ZW,)),
        ],
        compiler_params=pltpu.CompilerParams(collective_id=0, has_side_effects=True, vmem_limit_bytes=60 * 2**20),
    )(tensor, block_mask, group_row, green_occ, green_virt)


def dot(a, b):
    return jnp.dot(a, b, preferred_element_type=F32)


def iota(shape, dim):
    return lax.broadcasted_iota(jnp.int32, shape, dim)


def packed_kernel(
    tensor, mask, group, occ, virt, out,
    xin, xs, xr, xl, tb, me, occ_f, occ_t, vm, perms, sel, tabs, own_pos, half, ys, yr, yl, cb, sb, yrs, zf, zb, zr, spots,
    i_sem, x_send, x_recv, l_send, l_recv, t_sem, y_send, y_recv, c_send, c_recv, z_send, z_recv, s_sem,
):
    pa, mu = lax.axis_index("pa"), lax.axis_index("mu")
    x, z, core = pa // (2 * NZ), lax.rem(pa // 2, NZ), lax.rem(pa, 2)
    chip = x * NZ + z

    def moved(dx, dz):
        return lax.rem(x + dx + core * (dz - dx) + NX, NX), lax.rem(z + dz + core * (dx - dz) + NZ, NZ)

    def plane(x2, z2, c2):
        return ((x2 * NZ + z2) * 2 + c2, mu)

    def wait(ref, sem):
        pltpu.make_async_copy(ref, ref, sem).wait()

    def to_chips(source, target, send, recv):
        for dx, dz in NEAR:
            x2, z2 = moved(dx, dz)
            pltpu.make_async_remote_copy(
                src_ref=source(x2 * NZ + z2), dst_ref=target, send_sem=send, recv_sem=recv,
                device_id=plane(x2, z2, core), device_id_type=MESH,
            ).start()
        pltpu.make_async_copy(source(chip), target, recv).start()

    def tensor_chunk(w):
        return pltpu.make_async_copy(tensor.at[pl.ds(w * SR, SR)], tb.at[lax.rem(w, 2)], t_sem.at[lax.rem(w, 2)])

    def load_x(u, carry):
        g, a, b = u // 32, lax.rem(u // 4, 8), lax.rem(u, 4)
        pltpu.make_async_copy(
            tensor.at[pl.ds(g * 16, 16), pl.ds(pl.multiple_of(a * BS + mu * LB, LB), LB), pl.ds(pl.multiple_of(b * SB, SB), SB)],
            xin.at[u], i_sem,
        ).start()
        return carry

    lax.fori_loop(0, UNITS // 2, load_x, 0)
    tensor_chunk(0).start()
    barrier = pltpu.get_barrier_semaphore()
    for dx, dz in NEAR:
        pl.semaphore_signal(barrier, inc=1, device_id=plane(*moved(dx, dz), core), device_id_type=MESH)
    pl.semaphore_signal(barrier, inc=1, device_id=plane(x, z, 1 - core), device_id_type=MESH)
    for dy in DY:
        pl.semaphore_signal(barrier, inc=1, device_id=(pa, lax.rem(mu + dy, NY)), device_id_type=MESH)

    flat = jnp.zeros((NP // BS, 64), F32)
    for a in range(8):
        place = (iota((8, 64), 1) == iota((8, 64), 0) + 8 * a).astype(F32)
        flat += dot(mask[:, a, :].astype(F32), place)
    kept = jnp.zeros((2 * CHIPS, 256), F32)
    for g in range(3):
        rows = ((iota((2 * CHIPS, NP // BS), 0) * ROWS + 16 * g) // BS == iota((2 * CHIPS, NP // BS), 1)).astype(F32)
        place = (iota((64, 256), 1) == iota((64, 256), 0) + 64 * g).astype(F32)
        kept += dot(dot(rows, flat), place)
    upto = (iota((256, 256), 0) <= iota((256, 256), 1)).astype(F32)
    place_of = dot(kept, upto)
    own_pos[...] = place_of * kept
    order = place_of.astype(jnp.int32) - 1
    odd = lax.rem(iota((2 * CHIPS, 256), 1), 2)
    spot = order // 2 + jnp.where(lax.rem(order + 2, 2) == odd, 0, SLOTS)
    tabs[0 : 2 * CHIPS] = jnp.clip(jnp.where(kept > 0.5, spot, 2 * SLOTS), 0, 2 * SLOTS)
    taken = (own_pos[pl.ds(pa, 1), :] == (iota((256, 256), 0) + 1).astype(F32)).astype(F32)
    units = iota((8, 256), 1).astype(F32)
    unit = lax.dot_general(units, taken, (((1,), (1,)), ((), ())), preferred_element_type=F32).astype(jnp.int32)
    there = lax.dot_general(jnp.ones((8, 256), F32), taken, (((1,), (1,)), ((), ())), preferred_element_type=F32).astype(jnp.int32)
    tabs[2 * CHIPS : 2 * CHIPS + 8] = jnp.clip(unit // 2, 0, UNITS // 2 - 1)
    tabs[2 * CHIPS + 8 : 2 * CHIPS + 16] = jnp.clip(there * (1 + lax.rem(unit, 2)), 0, 2)
    to_smem = pltpu.make_async_copy(tabs, spots, s_sem)
    to_smem.start()

    to, at = iota((256, 256), 0), iota((256, 256), 1)
    perms[0] = (at == lax.rem(to, 16) * 16 + to // 16).astype(BF16)
    perms[1] = (at == (lax.rem(to, 8) * 2 + lax.rem(to // 8, 2)) * 16 + to // 16).astype(BF16)
    perms[2] = (at == lax.rem(to, 128) // 8 * 16 + to // 128 * 8 + lax.rem(to, 8)).astype(BF16)
    frm, into = iota((SB, SB), 0), iota((SB, SB), 1)
    for h in (0, 1):
        sel[0, h] = jnp.zeros((SB, SB), BF16)
        for b in (0, 1):
            sel[1 + b, h] = ((frm - BS * b == into - BS * h) & (into // BS == h)).astype(BF16)
    sel[3, 0] = (lax.rem(frm + BS, SB) == into).astype(BF16)

    to_smem.wait()
    wait(xin, i_sem)
    pl.semaphore_wait(barrier, CHIPS + NY - 1)

    def pack(w, carry):
        def one(i, carry):
            for k in range(3):
                r = w * (SLOTS // PW) + i * 3 + k
                full = jnp.zeros((256, SB), F32)
                for h in (0, 1):
                    cube = xin[spots[2 * CHIPS, 2 * r + h]].reshape(256, SB)
                    full += dot(cube, sel[spots[2 * CHIPS + 8, 2 * r + h], h])
                xs[:, r] = dot(perms[0], full.astype(BF16)).astype(BF16).reshape(16, 16, SB)
            return carry

        lax.fori_loop(0, SLOTS // PW // 3, one, 0)
        slots = pl.ds(w * (SLOTS // PW), SLOTS // PW)
        to_chips(lambda t: xs.at[t, slots], xr.at[chip, slots], x_send.at[w], x_recv.at[w])
        return carry

    lax.fori_loop(0, PW, pack, 0)

    spread = (block_of((NAO, 8), 0) == iota((NAO, 8), 1)).astype(F32)
    for g in range(3):
        rows = dot(spread, mask[(ROWS * pa + 16 * g) // BS].astype(F32))
        me[g] = lax.dot_general(rows, spread, (((1,), (1,)), ((), ())), preferred_element_type=F32).astype(BF16)
    group_row = group[...].astype(F32)
    row_group = jnp.sum(spread * group_row, axis=1, keepdims=True)
    col_group = lax.dot_general(group_row, spread, (((1,), (1,)), ((), ())), preferred_element_type=F32)
    near = jnp.abs(row_group - col_group) <= GROUP_REACH + 0.5
    vm[...] = jnp.where(near, virt[...].astype(F32), 0.0).astype(BF16)
    occ_f[...] = jnp.where(near, occ[...].astype(F32), 0.0).T
    for a in range(8):
        occ_t[a * LB : (a + 1) * LB] = occ_f[pl.ds(pl.multiple_of(a * BS + mu * LB, LB), LB), :].astype(BF16)

    def make_product(w, carry):
        for part in range(YR // SR):
            v = w * (YR // SR) + part
            tensor_chunk(v).wait()

            @pl.when(v + 1 < ROWS // SR)
            def _():
                tensor_chunk(v + 1).start()

            def one(p, carry):
                block = tb[lax.rem(v, 2), p] * me[w // 2]
                half[part * SR + p] = dot(occ_t[...], block).astype(BF16)
                return carry

            lax.fori_loop(0, SR, one, 0)
        for a in range(4):
            done = dot(half[:, a * 2 * LB : (a + 1) * 2 * LB, :].reshape(256, NAO), vm[...]).astype(BF16)
            ys[w, :, :, a * NAO : (a + 1) * NAO] = dot(perms[1], done).astype(BF16).reshape(16, 16, NAO)
        to_chips(lambda t: ys.at[w, t], yr.at[w, chip], y_send.at[w], y_recv.at[w])
        return carry

    lax.fori_loop(0, YW, make_product, 0)

    for w in range(PW):
        slots = pl.ds(w * (SLOTS // PW), SLOTS // PW)
        wait(xr.at[:, slots], x_recv.at[w])
    left_half = iota((16, SB), 1) < BS

    def unpack(i, carry):
        rows = dot(xr[i, 0:SLOTS].reshape(SLOTS * 16, SB), sel[3, 0])
        xr[i, SLOTS : 2 * SLOTS] = rows.astype(BF16).reshape(SLOTS, 16, SB)
        xr[i, 2 * SLOTS] = jnp.zeros((16, SB), BF16)
        j = 2 * i + core
        for g in range(3):
            row = pl.multiple_of(j * ROWS + g * 16, 16)
            for a in range(8):
                for b in range(4):
                    u = (g * 8 + a) * 8 + 2 * b
                    both = jnp.where(left_half, xr[i, spots[j, u]], xr[i, spots[j, u + 1]])
                    first = a % 2 * KC + a // 2 * NAO + b * SB
                    xl[pl.ds(row, 16), first : first + SB] = both
        rows = pl.ds(pl.multiple_of(j * ROWS, 16), ROWS)
        pltpu.make_async_remote_copy(
            src_ref=xl.at[rows], dst_ref=xl.at[rows], send_sem=l_send, recv_sem=l_recv,
            device_id=plane(x, z, 1 - core), device_id_type=MESH,
        ).start()
        return carry

    lax.fori_loop(0, CHIPS, unpack, 0)
    wait(xl.at[pl.ds(0, NP // 2)], l_recv)

    def partial(w, carry):
        wait(yr.at[w], y_recv.at[w])
        for k in range(4):
            rows = yr[w, :, :, k * NAO : (k + 1) * NAO].reshape(256, NAO)
            turned = dot(perms[2], rows).astype(BF16)
            yl[:, k * NAO : (k + 1) * NAO] = turned[:WR]
            yl[:, KC + k * NAO : KC + (k + 1) * NAO] = turned[WR:]

        def tile(y2):
            columns = xl[pl.ds(pl.multiple_of(y2 * QC, QC), QC), :]
            return lax.dot_general(yl[...], columns, (((1,), (1,)), ((), ())), preferred_element_type=F32)

        for k, dy in enumerate(DY):
            y2 = lax.rem(mu + dy, NY)
            cb[w, k] = tile(y2).astype(BF16)
            pltpu.make_async_remote_copy(
                src_ref=cb.at[w, k], dst_ref=yrs.at[w, k], send_sem=c_send.at[w], recv_sem=c_recv.at[w],
                device_id=(pa, y2), device_id_type=MESH,
            ).start()
        sb[lax.rem(w, 2)] = tile(mu)

        @pl.when(w > 0)
        def _():
            sum_y(w - 1)

        return carry

    def sum_y(w):
        wait(yrs.at[w], c_recv.at[w])
        total = (sb[lax.rem(w, 2)] + yrs[w, 0].astype(F32)) + (yrs[w, 1].astype(F32) + yrs[w, 2].astype(F32))
        for k in range(YZ):

            @pl.when(lax.rem(w, YZ) == k)
            def _():
                zf[:, k * YR : (k + 1) * YR, :] = total.reshape(CHIPS, YR, QC)

        @pl.when(lax.rem(w, YZ) == YZ - 1)
        def _():
            v = w // YZ
            zb[v] = zf[...].astype(BF16)
            to_chips(lambda t: zb.at[v, t], zr.at[v, chip], z_send.at[v], z_recv.at[v])

    lax.fori_loop(0, YW, partial, 0)
    sum_y(YW - 1)

    def finish(w, carry):
        wait(zr.at[w], z_recv.at[w])
        out[pl.ds(pl.multiple_of(w * ZR, ZR), ZR), :] = jnp.sum(zr[w].astype(F32), axis=0) * (1.0 / NAO)
        return carry

    lax.fori_loop(0, ZW, finish, 0)

    wait(xl.at[pl.ds(0, NP // 2)], l_send)
    for w in range(PW):
        wait(xs.at[pl.ds(0, CHIPS - 1), pl.ds(0, SLOTS // PW)], x_send.at[w])
    for w in range(YW):
        wait(yr.at[w, pl.ds(0, CHIPS - 1)], y_send.at[w])
        wait(cb.at[w], c_send.at[w])
    for w in range(ZW):
        wait(zr.at[w, pl.ds(0, CHIPS - 1)], z_send.at[w])


def packed(tensor, block_mask, group_row, green_occ, green_virt):
    vmem = pl.BlockSpec(memory_space=pltpu.VMEM)
    dma = pltpu.SemaphoreType.DMA
    return pl.pallas_call(
        packed_kernel,
        out_shape=jax.ShapeDtypeStruct((ROWS, QC), F32),
        in_specs=[pl.BlockSpec(memory_space=pl.ANY), vmem, vmem, vmem, vmem],
        out_specs=vmem,
        scratch_shapes=[
            pltpu.VMEM((UNITS // 2, 16, LB, SB), BF16),
            pltpu.VMEM((CHIPS, SLOTS, 16, SB), BF16),
            pltpu.VMEM((CHIPS, 2 * SLOTS + 1, 16, SB), BF16),
            pltpu.VMEM((NP, 2 * KC), BF16),
            pltpu.VMEM((2, SR, NAO, NAO), BF16),
            pltpu.VMEM((3, NAO, NAO), BF16),
            pltpu.VMEM((NAO, NAO), F32),
            pltpu.VMEM((SB, NAO), BF16),
            pltpu.VMEM((NAO, NAO), BF16),
            pltpu.VMEM((3, 256, 256), BF16),
            pltpu.VMEM((4, 2, SB, SB), BF16),
            pltpu.VMEM((2 * CHIPS + 16, 256), jnp.int32),
            pltpu.VMEM((2 * CHIPS, 256), F32),
            pltpu.VMEM((YR, SB, NAO), BF16),
            pltpu.VMEM((YW, CHIPS, 16, KC), BF16),
            pltpu.VMEM((YW, CHIPS, 16, KC), BF16),
            pltpu.VMEM((WR, 2 * KC), BF16),
            pltpu.VMEM((YW, NY - 1, WR, QC), BF16),
            pltpu.VMEM((2, WR, QC), F32),
            pltpu.VMEM((YW, NY - 1, WR, QC), BF16),
            pltpu.VMEM((CHIPS, ZR, QC), F32),
            pltpu.VMEM((ZW, CHIPS, ZR, QC), BF16),
            pltpu.VMEM((ZW, CHIPS, ZR, QC), BF16),
            pltpu.SMEM((2 * CHIPS + 16, 256), jnp.int32),
            dma, dma((PW,)), dma((PW,)), dma, dma, dma((2,)), dma((YW,)), dma((YW,)), dma((YW,)), dma((YW,)), dma((ZW,)), dma((ZW,)), dma,
        ],
        compiler_params=pltpu.CompilerParams(collective_id=1, has_side_effects=True, vmem_limit_bytes=62 * 2**20),
    )(tensor, block_mask, group_row, green_occ, green_virt)


def shards(tensor, block_mask, group_of_block, green_occ, green_virt):
    kept = jnp.sum(block_mask, axis=(1, 2)).reshape(NP // BS // 3, 3)
    a, b, c = kept[:, 0], kept[:, 1], kept[:, 2]
    most = jnp.max(jnp.maximum(jnp.maximum(3 * a, a + 2 * b), jnp.maximum(2 * b + c, 3 * c)))
    return lax.cond(
        most <= 2 * SLOTS, packed, whole, tensor, block_mask, group_of_block.reshape(1, 8), green_occ, green_virt
    )


def solution(mesh):
    placed = (P("pa", None, None), P(), P(), P(), P())
    return jax.shard_map(shards, mesh=mesh, in_specs=placed, out_specs=P("pa", "mu"), check_vma=False)
```

```python
import functools

import jax
import jax.numpy as jnp
from jax import lax
from jax.experimental import pallas as pl
from jax.experimental.pallas import tpu as pltpu
from jax.sharding import PartitionSpec as P

MESH = pl.DeviceIdType.MESH
F32, BF16 = jnp.float32, jnp.bfloat16

BS = 64
GROUP_REACH = 1
NX = NZ = NY = 4
CHIPS = NX * NZ
ROWS = 48
NP = 1536
NAO = 512
LB = 16
SB = 128
KC = LB * SB
XW = 3
XR = ROWS // XW
YW = 6
YR = ROWS // YW
TR = 8
ZW = 3
ZR = ROWS // ZW
YZ = ZR // YR
WR = CHIPS * YR
QC = NP // NY
NEAR = [(1, 0), (0, 1), (-1, 0), (0, -1), (1, 1), (-1, -1), (1, -1), (-1, 1), (2, 0), (0, 2), (2, 1), (1, 2), (2, -1), (-1, 2), (2, 2)]
DY = (2, 1, 3)


TIERS = (42, 46, 52, 60)
EARLY = (4, 10)
UNITS = 3 * 64
SR = 4


def block_of(shape, dim, first=0):
    return lax.broadcasted_iota(jnp.int32, shape, dim) // BS + first


def kernel(
    tensor, mask, group, occ, virt, out,
    xr, xl, tb, me, occ_t, vm, mv, perm, half, ys, yr, yl, cb, sb, yrs, zf, zb, zr,
    x_send, x_recv, l_send, l_recv, t_sem, y_send, y_recv, c_send, c_recv, z_send, z_recv,
):
    pa, mu = lax.axis_index("pa"), lax.axis_index("mu")
    x, z, core = pa // (2 * NZ), lax.rem(pa // 2, NZ), lax.rem(pa, 2)
    chip = x * NZ + z

    def moved(dx, dz):
        return lax.rem(x + dx + core * (dz - dx) + NX, NX), lax.rem(z + dz + core * (dx - dz) + NZ, NZ)

    def plane(x2, z2, c2):
        return ((x2 * NZ + z2) * 2 + c2, mu)

    def tensor_chunk(w):
        return pltpu.make_async_copy(tensor.at[pl.ds(w * TR, TR)], tb.at[lax.rem(w, 2)], t_sem.at[lax.rem(w, 2)])

    tensor_chunk(0).start()
    barrier = pltpu.get_barrier_semaphore()
    for c2 in (0, 1):
        for dx, dz in NEAR + [(0, 0)]:
            if (dx, dz, c2) != (0, 0, 0):
                pl.semaphore_signal(barrier, inc=1, device_id=plane(*moved(dx, dz), lax.rem(core + c2, 2)), device_id_type=MESH)
    for dy in DY:
        pl.semaphore_signal(barrier, inc=1, device_id=(pa, lax.rem(mu + dy, NY)), device_id_type=MESH)
    pl.semaphore_wait(barrier, 2 * CHIPS - 1 + NY - 1)

    def send_x(w, carry):
        def part(x2, z2, c2):
            return tensor.at[
                pl.ds(w * XR, XR),
                pl.ds(pl.multiple_of(mu * (NAO // NY) + x2 * 2 * LB + c2 * LB, LB), LB),
                pl.ds(pl.multiple_of(z2 * SB, SB), SB),
            ]

        for c2 in (0, 1):
            for dx, dz in NEAR + [(0, 0)]:
                where = (*moved(dx, dz), lax.rem(core + c2, 2))
                if (dx, dz, c2) == (0, 0, 0):
                    pltpu.make_async_copy(part(*where), xr.at[w, pa], x_recv.at[w]).start()
                else:
                    pltpu.make_async_remote_copy(
                        src_ref=part(*where), dst_ref=xr.at[w, pa], send_sem=x_send.at[w], recv_sem=x_recv.at[w],
                        device_id=plane(*where), device_id_type=MESH,
                    ).start()
        return carry

    lax.fori_loop(0, XW, send_x, 0)

    spread = (block_of((NAO, 8), 0) == lax.broadcasted_iota(jnp.int32, (NAO, 8), 1)).astype(F32)
    for g in range(3):
        blocks = mask[(ROWS * pa + 16 * g) // BS].astype(F32)
        rows = jnp.dot(spread, blocks, preferred_element_type=F32)
        me[g] = lax.dot_general(rows, spread, (((1,), (1,)), ((), ())), preferred_element_type=F32).astype(BF16)
    lane_block = lax.broadcasted_iota(jnp.int32, (8, SB), 0) == block_of((8, SB), 1, 2 * z)
    own_blocks = mask[:, pl.ds(2 * mu + x // 2, 1), :].astype(F32).reshape(NP // BS, 8)
    mv[...] = jnp.dot(own_blocks, lane_block.astype(F32), preferred_element_type=F32)
    group_row = group[...].astype(F32)
    row_group = jnp.sum(spread * group_row, axis=1, keepdims=True)
    col_group = lax.dot_general(group_row, spread, (((1,), (1,)), ((), ())), preferred_element_type=F32)
    vm[...] = jnp.where(jnp.abs(row_group - col_group) <= GROUP_REACH + 0.5, virt[...].astype(F32), 0.0).astype(BF16)
    occ_block = lax.broadcasted_iota(jnp.int32, (8, SB), 0) == block_of((8, SB), 1, 2 * mu)
    occ_group = jnp.dot(group_row, occ_block.astype(F32), preferred_element_type=F32)
    occ_cols = occ[:, pl.ds(pl.multiple_of(mu * SB, SB), SB)].astype(F32)
    occ_cols = jnp.where(jnp.abs(row_group - occ_group) <= GROUP_REACH + 0.5, occ_cols, 0.0)
    occ_t[...] = occ_cols.T.astype(BF16)
    to = lax.broadcasted_iota(jnp.int32, (256, 256), 0)
    perm[...] = (lax.broadcasted_iota(jnp.int32, (256, 256), 1) == lax.rem(to, 16) * 16 + to // 16).astype(BF16)

    def send_y(w):
        def part(x2, z2):
            return ys.at[pl.ds(w * YR, YR), pl.ds(pl.multiple_of(x2 * 2 * LB, 2 * LB), 2 * LB), pl.ds(pl.multiple_of(z2 * SB, SB), SB)]

        for dx, dz in NEAR:
            x2, z2 = moved(dx, dz)
            pltpu.make_async_remote_copy(
                src_ref=part(x2, z2), dst_ref=yr.at[w, chip], send_sem=y_send.at[w], recv_sem=y_recv.at[w],
                device_id=plane(x2, z2, core), device_id_type=MESH,
            ).start()
        pltpu.make_async_copy(part(x, z), yr.at[w, chip], y_recv.at[w]).start()

    def make_product(w, carry):
        tensor_chunk(w).wait()

        @pl.when(w + 1 < ROWS // TR)
        def _():
            tensor_chunk(w + 1).start()

        slot = lax.rem(w, 2)

        def one(p, carry):
            block = tb[slot, p] * me[w // 2]
            half[pl.ds(pl.multiple_of(p * SB, SB), SB), :] = jnp.dot(occ_t[...], block, preferred_element_type=F32).astype(BF16)
            return carry

        lax.fori_loop(0, TR, one, 0)

        def two(i, carry):
            rows = half[pl.ds(pl.multiple_of(i * 2 * SB, 2 * SB), 2 * SB), :]
            done = jnp.dot(rows, vm[...], preferred_element_type=F32).astype(BF16)
            ys[pl.ds(w * TR + 2 * i, 2)] = done.reshape(2, SB, NAO)
            return carry

        lax.fori_loop(0, TR // 2, two, 0)
        for k in range(TR // YR):
            send_y(w * (TR // YR) + k)
        return carry

    lax.fori_loop(0, ROWS // TR, make_product, 0)

    def sibling(rows, columns):
        return pltpu.make_async_remote_copy(
            src_ref=xl.at[rows, columns], dst_ref=xl.at[rows, columns], send_sem=l_send, recv_sem=l_recv,
            device_id=plane(x, z, 1 - core), device_id_type=MESH,
        )

    own = pl.multiple_of(core * KC, KC)
    other = pl.multiple_of((1 - core) * KC, KC)

    def turn(rows):
        return jnp.dot(perm[...], rows, preferred_element_type=F32).astype(BF16).reshape(16, 16, SB)

    def lay_x(w, carry):
        pltpu.make_async_copy(xr.at[w], xr.at[w], x_recv.at[w]).wait()

        def one(j, carry):
            row = pl.multiple_of(j * ROWS + w * XR, XR)
            keep = mv[pl.ds(row // BS, 1), :].astype(BF16)
            turned = turn(xr[w, j].reshape(256, SB) * keep)
            for i in range(LB):
                xl[pl.ds(row, XR), pl.ds(pl.multiple_of(own + i * SB, SB), SB)] = turned[i]
            sibling(pl.ds(row, XR), pl.ds(own, KC)).start()
            return carry

        lax.fori_loop(0, 2 * CHIPS, one, 0)
        return carry

    lax.fori_loop(0, XW, lay_x, 0)
    pltpu.make_async_copy(xl.at[:, pl.ds(other, KC)], xl.at[:, pl.ds(other, KC)], l_recv).wait()

    def partial(w, carry):
        pltpu.make_async_copy(yr.at[w], yr.at[w], y_recv.at[w]).wait()

        def lay_y(i, carry):
            for h in (0, 1):
                turned = turn(yr[w, pl.ds(16 // YR * i, 16 // YR), :, h * LB : (h + 1) * LB, :].reshape(256, SB))
                for k in range(LB):
                    yl[pl.ds(pl.multiple_of(i * 16, 16), 16), (h * LB + k) * SB : (h * LB + k + 1) * SB] = turned[k]
            return carry

        lax.fori_loop(0, WR // 16, lay_y, 0)

        def tile(y2):
            columns = xl[pl.ds(pl.multiple_of(y2 * QC, QC), QC), :]
            return lax.dot_general(yl[...], columns, (((1,), (1,)), ((), ())), preferred_element_type=F32)

        for k, dy in enumerate(DY):
            y2 = lax.rem(mu + dy, NY)
            cb[w, k] = tile(y2).astype(BF16)
            pltpu.make_async_remote_copy(
                src_ref=cb.at[w, k], dst_ref=yrs.at[w, k], send_sem=c_send.at[w], recv_sem=c_recv.at[w],
                device_id=(pa, y2), device_id_type=MESH,
            ).start()
        sb[lax.rem(w, 2)] = tile(mu)

        @pl.when(w > 0)
        def _():
            sum_y(w - 1)

        return carry

    def sum_y(w):
        pltpu.make_async_copy(yrs.at[w], yrs.at[w], c_recv.at[w]).wait()
        total = (sb[lax.rem(w, 2)] + yrs[w, 0].astype(F32)) + (yrs[w, 1].astype(F32) + yrs[w, 2].astype(F32))
        for k in range(YZ):

            @pl.when(lax.rem(w, YZ) == k)
            def _():
                zf[:, k * YR : (k + 1) * YR, :] = total.reshape(CHIPS, YR, QC)

        @pl.when(lax.rem(w, YZ) == YZ - 1)
        def _():
            send_z(w // YZ)

    def send_z(v):
        zb[v] = zf[...].astype(BF16)
        for dx, dz in NEAR:
            x2, z2 = moved(dx, dz)
            pltpu.make_async_remote_copy(
                src_ref=zb.at[v, x2 * NZ + z2], dst_ref=zr.at[v, chip], send_sem=z_send.at[v], recv_sem=z_recv.at[v],
                device_id=plane(x2, z2, core), device_id_type=MESH,
            ).start()
        pltpu.make_async_copy(zb.at[v, chip], zr.at[v, chip], z_recv.at[v]).start()

    lax.fori_loop(0, YW, partial, 0)
    sum_y(YW - 1)

    def finish(w, carry):
        pltpu.make_async_copy(zr.at[w], zr.at[w], z_recv.at[w]).wait()
        out[pl.ds(pl.multiple_of(w * ZR, ZR), ZR), :] = jnp.sum(zr[w].astype(F32), axis=0) * (1.0 / NAO)
        return carry

    lax.fori_loop(0, ZW, finish, 0)

    def left(ref, sem):
        pltpu.make_async_copy(ref, ref, sem).wait()

    left(xl.at[:, pl.ds(own, KC)], l_send)
    for w in range(XW):
        left(xr.at[w, pl.ds(0, 2 * CHIPS - 1)], x_send.at[w])
    for w in range(YW):
        left(yr.at[w, pl.ds(0, CHIPS - 1)], y_send.at[w])
        left(cb.at[w], c_send.at[w])
    for w in range(ZW):
        left(zr.at[w, pl.ds(0, CHIPS - 1)], z_send.at[w])


def whole(tensor, block_mask, group_row, green_occ, green_virt):
    vmem = pl.BlockSpec(memory_space=pltpu.VMEM)
    dma = pltpu.SemaphoreType.DMA
    return pl.pallas_call(
        kernel,
        out_shape=jax.ShapeDtypeStruct((ROWS, QC), F32),
        in_specs=[pl.BlockSpec(memory_space=pl.ANY), vmem, vmem, vmem, vmem],
        out_specs=vmem,
        scratch_shapes=[
            pltpu.VMEM((XW, 2 * CHIPS, XR, LB, SB), BF16),
            pltpu.VMEM((NP, 2 * KC), BF16),
            pltpu.VMEM((2, TR, NAO, NAO), BF16),
            pltpu.VMEM((3, NAO, NAO), BF16),
            pltpu.VMEM((SB, NAO), BF16),
            pltpu.VMEM((NAO, NAO), BF16),
            pltpu.VMEM((NP // BS, SB), F32),
            pltpu.VMEM((256, 256), BF16),
            pltpu.VMEM((TR * SB, NAO), BF16),
            pltpu.VMEM((ROWS, SB, NAO), BF16),
            pltpu.VMEM((YW, CHIPS, YR, 2 * LB, SB), BF16),
            pltpu.VMEM((WR, 2 * KC), BF16),
            pltpu.VMEM((YW, NY - 1, WR, QC), BF16),
            pltpu.VMEM((2, WR, QC), F32),
            pltpu.VMEM((YW, NY - 1, WR, QC), BF16),
            pltpu.VMEM((CHIPS, ZR, QC), F32),
            pltpu.VMEM((ZW, CHIPS, ZR, QC), BF16),
            pltpu.VMEM((ZW, CHIPS, ZR, QC), BF16),
            dma((XW,)), dma((XW,)), dma, dma, dma((2,)), dma((YW,)), dma((YW,)), dma((YW,)), dma((YW,)), dma((ZW,)), dma((ZW,)),
        ],
        compiler_params=pltpu.CompilerParams(collective_id=0, has_side_effects=True, vmem_limit_bytes=60 * 2**20),
    )(tensor, block_mask, group_row, green_occ, green_virt)


def granule_rows(chip, core):
    odd = lax.rem(chip, 2)
    gives = 2 - odd - core
    first = jnp.where(gives == 0, 1, 0)
    second = jnp.where(gives == 2, 1, 2)
    row = chip * (2 * ROWS)
    return row + core * ROWS + first * 16, row + core * ROWS + second * 16, row + (4 - 2 * core - odd) * 16, row + core * ROWS + gives * 16


def slot_waves(slots):
    late = slots - sum(EARLY)
    third = late // 4 * 2
    return *EARLY, third, late - third


def dot(a, b):
    return jnp.dot(a, b, preferred_element_type=F32)


def iota(shape, dim):
    return lax.broadcasted_iota(jnp.int32, shape, dim)


def packed_kernel(
    slots,
    tensor, mask, group, occ, virt, out,
    xa, xb, xs, xr, xl, tb, me, occ_f, occ_t, vm, perms, sel, tabs, own_pos, half, ys, yr, yl, cb, sb, yrs, zf, zb, zr, spots,
    i_sem, e_send, e_recv, x_send, x_recv, l_send, l_recv, t_sem, y_send, y_recv, c_send, c_recv, z_send, z_recv, s_sem,
):
    pa, mu = lax.axis_index("pa"), lax.axis_index("mu")
    x, z, core = pa // (2 * NZ), lax.rem(pa // 2, NZ), lax.rem(pa, 2)
    chip = x * NZ + z

    def moved(dx, dz):
        return lax.rem(x + dx + core * (dz - dx) + NX, NX), lax.rem(z + dz + core * (dx - dz) + NZ, NZ)

    def plane(x2, z2, c2):
        return ((x2 * NZ + z2) * 2 + c2, mu)

    def wait(ref, sem):
        pltpu.make_async_copy(ref, ref, sem).wait()

    def to_chips(source, target, send, recv):
        for dx, dz in NEAR:
            x2, z2 = moved(dx, dz)
            pltpu.make_async_remote_copy(
                src_ref=source(x2 * NZ + z2), dst_ref=target, send_sem=send, recv_sem=recv,
                device_id=plane(x2, z2, core), device_id_type=MESH,
            ).start()
        pltpu.make_async_copy(source(chip), target, recv).start()

    def tensor_chunk(w):
        return pltpu.make_async_copy(tensor.at[pl.ds(w * SR, SR)], tb.at[lax.rem(w, 2)], t_sem.at[lax.rem(w, 2)])

    own_rows = granule_rows(chip, core)

    def x_block(granule, v):
        a, b = v // 4, lax.rem(v, 4)
        row = pl.multiple_of(own_rows[granule] - pa * ROWS, 16)
        return tensor.at[pl.ds(row, 16), pl.ds(pl.multiple_of(a * BS + mu * LB, LB), LB), pl.ds(pl.multiple_of(b * SB, SB), SB)]

    def load_x(v, carry):
        for g in (0, 1):
            pltpu.make_async_copy(x_block(g, v), xa.at[g * 32 + v], i_sem).start()
        return carry

    lax.fori_loop(0, 32, load_x, 0)
    tensor_chunk(0).start()
    barrier = pltpu.get_barrier_semaphore()
    for dx, dz in NEAR:
        pl.semaphore_signal(barrier, inc=1, device_id=plane(*moved(dx, dz), core), device_id_type=MESH)
    pl.semaphore_signal(barrier, inc=1, device_id=plane(x, z, 1 - core), device_id_type=MESH)
    for dy in DY:
        pl.semaphore_signal(barrier, inc=1, device_id=(pa, lax.rem(mu + dy, NY)), device_id_type=MESH)
    pl.semaphore_wait(barrier, CHIPS + NY - 1)

    def give_x(v, carry):
        pltpu.make_async_remote_copy(
            src_ref=x_block(3, v), dst_ref=xb.at[v], send_sem=e_send, recv_sem=e_recv,
            device_id=plane(x, z, 1 - core), device_id_type=MESH,
        ).start()
        return carry

    lax.fori_loop(0, 32, give_x, 0)

    sizes = slot_waves(slots)
    starts = [sum(sizes[:w]) for w in range(len(sizes))]

    by_block = mask[...].astype(F32).reshape(64, NP // BS).astype(BF16)
    kept = jnp.zeros((2 * CHIPS, 256), F32)
    for g in range(3):
        device = iota((2 * CHIPS, NP // BS), 0)
        first_row = granule_rows(device // 2, lax.rem(device, 2))[g]
        rows = (first_row // BS == iota((2 * CHIPS, NP // BS), 1)).astype(F32).astype(BF16)
        units = lax.dot_general(rows, by_block, (((1,), (1,)), ((), ())), preferred_element_type=F32).astype(BF16)
        place = (iota((64, 256), 1) == iota((64, 256), 0) + 64 * g).astype(F32).astype(BF16)
        kept += dot(units, place)
    upto = (iota((256, 256), 0) <= iota((256, 256), 1)).astype(F32).astype(BF16)
    place_of = dot(kept.astype(BF16), upto)
    ours = jnp.sum(jnp.where(iota((2 * CHIPS, 256), 1) < 128, kept, 0.0), axis=1, keepdims=True)
    place_of += jnp.where(iota((2 * CHIPS, 256), 1) < 128, 0.0, jnp.maximum(2 * sum(EARLY) - ours, 0.0))
    own_pos[...] = place_of * kept
    order = place_of.astype(jnp.int32) - 1
    odd = lax.rem(iota((2 * CHIPS, 256), 1), 2)
    spot = order // 2 + jnp.where(lax.rem(order + 2, 2) == odd, 0, slots)
    tabs[0 : 2 * CHIPS] = jnp.clip(jnp.where(kept > 0.5, spot, 2 * slots), 0, 2 * slots)
    taken = (own_pos[pl.ds(pa, 1), :] == (iota((256, 256), 0) + 1).astype(F32)).astype(F32).astype(BF16)
    units = iota((8, 256), 1).astype(F32).astype(BF16)
    unit = lax.dot_general(units, taken, (((1,), (1,)), ((), ())), preferred_element_type=F32).astype(jnp.int32)
    there = lax.dot_general(jnp.ones((8, 256), BF16), taken, (((1,), (1,)), ((), ())), preferred_element_type=F32).astype(jnp.int32)
    tabs[2 * CHIPS : 2 * CHIPS + 8] = jnp.clip(unit // 2, 0, 63)
    tabs[2 * CHIPS + 16 : 2 * CHIPS + 24] = unit // 128
    tabs[2 * CHIPS + 24 : 2 * CHIPS + 32] = jnp.clip(unit // 2 - 64, 0, 31)
    tabs[2 * CHIPS + 8 : 2 * CHIPS + 16] = jnp.clip(there * (1 + lax.rem(unit, 2)), 0, 2)
    to_smem = pltpu.make_async_copy(tabs, spots, s_sem)
    to_smem.start()

    to, at = iota((256, 256), 0), iota((256, 256), 1)
    perms[0] = (at == lax.rem(to, 16) * 16 + to // 16).astype(BF16)
    perms[1] = (at == (lax.rem(to, 8) * 2 + lax.rem(to // 8, 2)) * 16 + to // 16).astype(BF16)
    perms[2] = (at == lax.rem(to, 128) // 8 * 16 + to // 128 * 8 + lax.rem(to, 8)).astype(BF16)
    frm, into = iota((SB, SB), 0), iota((SB, SB), 1)
    for h in (0, 1):
        sel[0, h] = jnp.zeros((SB, SB), BF16)
        for b in (0, 1):
            sel[1 + b, h] = ((frm - BS * b == into - BS * h) & (into // BS == h)).astype(BF16)
    sel[3, 0] = (lax.rem(frm + BS, SB) == into).astype(BF16)

    to_smem.wait()
    wait(xa, i_sem)

    for w, n in enumerate(sizes):
        if w == len(EARLY):
            wait(xb, e_recv)

        def one(i, carry):
            for k in range(2):
                r = starts[w] + i * 2 + k
                full = jnp.zeros((256, SB), F32)
                for h in (0, 1):
                    cube = xa[spots[2 * CHIPS, 2 * r + h]]
                    if w >= len(EARLY):
                        cube = jnp.where(spots[2 * CHIPS + 16, 2 * r + h] > 0, xb[spots[2 * CHIPS + 24, 2 * r + h]], cube)
                    cube = cube.reshape(256, SB)
                    full += dot(cube, sel[spots[2 * CHIPS + 8, 2 * r + h], h])
                xs[:, r] = dot(perms[0], full.astype(BF16)).astype(BF16).reshape(16, 16, SB)
            return carry

        lax.fori_loop(0, n // 2, one, 0)
        part = pl.ds(starts[w], n)
        to_chips(lambda t: xs.at[t, part], xr.at[chip, part], x_send.at[w], x_recv.at[w])

    spread = (block_of((NAO, 8), 0) == iota((NAO, 8), 1)).astype(F32)
    for g in range(3):
        this = iota((8, 8, NP // BS), 2) == (ROWS * pa + 16 * g) // BS
        rows = dot(spread, jnp.sum(jnp.where(this, mask[...].astype(F32), 0.0), axis=2))
        me[g] = lax.dot_general(rows, spread, (((1,), (1,)), ((), ())), preferred_element_type=F32).astype(BF16)
    group_row = group[...].astype(F32)
    row_group = jnp.sum(spread * group_row, axis=1, keepdims=True)
    col_group = lax.dot_general(group_row, spread, (((1,), (1,)), ((), ())), preferred_element_type=F32)
    near = jnp.abs(row_group - col_group) <= GROUP_REACH + 0.5
    vm[...] = jnp.where(near, virt[...].astype(F32), 0.0).astype(BF16)
    occ_f[...] = jnp.where(near, occ[...].astype(F32), 0.0).T
    for a in range(8):
        occ_t[a * LB : (a + 1) * LB] = occ_f[pl.ds(pl.multiple_of(a * BS + mu * LB, LB), LB), :].astype(BF16)

    def make_product(w, carry):
        for part in range(YR // SR):
            v = w * (YR // SR) + part
            tensor_chunk(v).wait()

            @pl.when(v + 1 < ROWS // SR)
            def _():
                tensor_chunk(v + 1).start()

            def one(p, carry):
                block = tb[lax.rem(v, 2), p] * me[w // 2]
                half[part * SR + p] = dot(occ_t[...], block).astype(BF16)
                return carry

            lax.fori_loop(0, SR, one, 0)
        for a in range(4):
            done = dot(half[:, a * 2 * LB : (a + 1) * 2 * LB, :].reshape(256, NAO), vm[...]).astype(BF16)
            ys[w, :, :, a * NAO : (a + 1) * NAO] = dot(perms[1], done).astype(BF16).reshape(16, 16, NAO)
        to_chips(lambda t: ys.at[w, t], yr.at[w, chip], y_send.at[w], y_recv.at[w])
        return carry

    lax.fori_loop(0, YW, make_product, 0)

    for w, n in enumerate(sizes):
        wait(xr.at[:, pl.ds(starts[w], n)], x_recv.at[w])
    left_half = iota((16, SB), 1) < BS

    def unpack(i, carry):
        rows = dot(xr[i, 0:slots].reshape(slots * 16, SB), sel[3, 0])
        xr[i, slots : 2 * slots] = rows.astype(BF16).reshape(slots, 16, SB)
        xr[i, 2 * slots] = jnp.zeros((16, SB), BF16)
        j = 2 * i + core
        for g in range(3):
            row = pl.multiple_of(granule_rows(i, core)[g], 16)
            for a in range(8):
                for b in range(4):
                    u = (g * 8 + a) * 8 + 2 * b
                    both = jnp.where(left_half, xr[i, spots[j, u]], xr[i, spots[j, u + 1]])
                    first = a % 2 * KC + a // 2 * NAO + b * SB
                    xl[pl.ds(row, 16), first : first + SB] = both
            rows = pl.ds(row, 16)
            pltpu.make_async_remote_copy(
                src_ref=xl.at[rows], dst_ref=xl.at[rows], send_sem=l_send, recv_sem=l_recv,
                device_id=plane(x, z, 1 - core), device_id_type=MESH,
            ).start()
        return carry

    lax.fori_loop(0, CHIPS, unpack, 0)
    wait(xl.at[pl.ds(0, NP // 2)], l_recv)

    def partial(w, carry):
        wait(yr.at[w], y_recv.at[w])
        for k in range(4):
            rows = yr[w, :, :, k * NAO : (k + 1) * NAO].reshape(256, NAO)
            turned = dot(perms[2], rows).astype(BF16)
            yl[:, k * NAO : (k + 1) * NAO] = turned[:WR]
            yl[:, KC + k * NAO : KC + (k + 1) * NAO] = turned[WR:]

        def tile(y2):
            columns = xl[pl.ds(pl.multiple_of(y2 * QC, QC), QC), :]
            return lax.dot_general(yl[...], columns, (((1,), (1,)), ((), ())), preferred_element_type=F32)

        for k, dy in enumerate(DY):
            y2 = lax.rem(mu + dy, NY)
            cb[w, k] = tile(y2).astype(BF16)
            pltpu.make_async_remote_copy(
                src_ref=cb.at[w, k], dst_ref=yrs.at[w, k], send_sem=c_send.at[w], recv_sem=c_recv.at[w],
                device_id=(pa, y2), device_id_type=MESH,
            ).start()
        sb[lax.rem(w, 2)] = tile(mu)

        @pl.when(w > 0)
        def _():
            sum_y(w - 1)

        return carry

    def sum_y(w):
        wait(yrs.at[w], c_recv.at[w])
        total = (sb[lax.rem(w, 2)] + yrs[w, 0].astype(F32)) + (yrs[w, 1].astype(F32) + yrs[w, 2].astype(F32))
        for k in range(YZ):

            @pl.when(lax.rem(w, YZ) == k)
            def _():
                zf[:, k * YR : (k + 1) * YR, :] = total.reshape(CHIPS, YR, QC)

        @pl.when(lax.rem(w, YZ) == YZ - 1)
        def _():
            v = w // YZ
            zb[v] = zf[...].astype(BF16)
            to_chips(lambda t: zb.at[v, t], zr.at[v, chip], z_send.at[v], z_recv.at[v])

    lax.fori_loop(0, YW, partial, 0)
    sum_y(YW - 1)

    def finish(w, carry):
        wait(zr.at[w], z_recv.at[w])
        out[pl.ds(pl.multiple_of(w * ZR, ZR), ZR), :] = jnp.sum(zr[w].astype(F32), axis=0) * (1.0 / NAO)
        return carry

    lax.fori_loop(0, ZW, finish, 0)

    wait(xb, e_send)
    wait(xl.at[pl.ds(0, NP // 2)], l_send)
    for w, n in enumerate(sizes):
        wait(xs.at[pl.ds(0, CHIPS - 1), pl.ds(0, n)], x_send.at[w])
    for w in range(YW):
        wait(yr.at[w, pl.ds(0, CHIPS - 1)], y_send.at[w])
        wait(cb.at[w], c_send.at[w])
    for w in range(ZW):
        wait(zr.at[w, pl.ds(0, CHIPS - 1)], z_send.at[w])


def packed(tier, tensor, block_mask, group_row, green_occ, green_virt):
    slots = TIERS[tier]
    waves = len(slot_waves(slots))
    vmem = pl.BlockSpec(memory_space=pltpu.VMEM)
    dma = pltpu.SemaphoreType.DMA
    return pl.pallas_call(
        functools.partial(packed_kernel, slots),
        out_shape=jax.ShapeDtypeStruct((ROWS, QC), F32),
        in_specs=[pl.BlockSpec(memory_space=pl.ANY), vmem, vmem, vmem, vmem],
        out_specs=vmem,
        scratch_shapes=[
            pltpu.VMEM((64, 16, LB, SB), BF16),
            pltpu.VMEM((32, 16, LB, SB), BF16),
            pltpu.VMEM((CHIPS, slots, 16, SB), BF16),
            pltpu.VMEM((CHIPS, 2 * slots + 1, 16, SB), BF16),
            pltpu.VMEM((NP, 2 * KC), BF16),
            pltpu.VMEM((2, SR, NAO, NAO), BF16),
            pltpu.VMEM((3, NAO, NAO), BF16),
            pltpu.VMEM((NAO, NAO), F32),
            pltpu.VMEM((SB, NAO), BF16),
            pltpu.VMEM((NAO, NAO), BF16),
            pltpu.VMEM((3, 256, 256), BF16),
            pltpu.VMEM((4, 2, SB, SB), BF16),
            pltpu.VMEM((2 * CHIPS + 32, 256), jnp.int32),
            pltpu.VMEM((2 * CHIPS, 256), F32),
            pltpu.VMEM((YR, SB, NAO), BF16),
            pltpu.VMEM((YW, CHIPS, 16, KC), BF16),
            pltpu.VMEM((YW, CHIPS, 16, KC), BF16),
            pltpu.VMEM((WR, 2 * KC), BF16),
            pltpu.VMEM((YW, NY - 1, WR, QC), BF16),
            pltpu.VMEM((2, WR, QC), F32),
            pltpu.VMEM((YW, NY - 1, WR, QC), BF16),
            pltpu.VMEM((CHIPS, ZR, QC), F32),
            pltpu.VMEM((ZW, CHIPS, ZR, QC), BF16),
            pltpu.VMEM((ZW, CHIPS, ZR, QC), BF16),
            pltpu.SMEM((2 * CHIPS + 32, 256), jnp.int32),
            dma, dma, dma, dma((waves,)), dma((waves,)), dma, dma, dma((2,)), dma((YW,)), dma((YW,)), dma((YW,)), dma((YW,)), dma((ZW,)), dma((ZW,)), dma,
        ],
        compiler_params=pltpu.CompilerParams(collective_id=1 + tier, has_side_effects=True, vmem_limit_bytes=62 * 2**20),
    )(tensor, jnp.transpose(block_mask, (1, 2, 0)), group_row, green_occ, green_virt)


def shards(tensor, block_mask, group_of_block, green_occ, green_virt):
    kept = jnp.sum(block_mask, axis=(1, 2)).reshape(NP // BS // 3, 3)
    a, b, c = kept[:, 0], kept[:, 1], kept[:, 2]
    most = 0
    for keeps, gets in ((2 * a, b), (a + b, a), (b + c, c), (2 * c, b)):
        most = jnp.maximum(most, jnp.maximum(keeps, 2 * sum(EARLY)) + gets)
    most = jnp.max(most)
    branches = [functools.partial(packed, tier) for tier in range(len(TIERS))] + [whole]
    which = sum((most > 2 * slots).astype(jnp.int32) for slots in TIERS)
    return lax.switch(which, branches, tensor, block_mask, group_of_block.reshape(1, 8), green_occ, green_virt)


def solution(mesh):
    placed = (P("pa", None, None), P(), P(), P(), P())
    return jax.shard_map(shards, mesh=mesh, in_specs=placed, out_specs=P("pa", "mu"), check_vma=False)
```

```python
import functools

import jax
import jax.numpy as jnp
from jax import lax
from jax.experimental import pallas as pl
from jax.experimental.pallas import tpu as pltpu
from jax.sharding import PartitionSpec as P

MESH = pl.DeviceIdType.MESH
F32, BF16 = jnp.float32, jnp.bfloat16

BS = 64
GROUP_REACH = 1
NX = NZ = NY = 4
CHIPS = NX * NZ
ROWS = 48
NP = 1536
NAO = 512
LB = 16
SB = 128
KC = LB * SB
XW = 3
XR = ROWS // XW
YW = 6
YR = ROWS // YW
TR = 8
ZW = 3
ZR = ROWS // ZW
YZ = ZR // YR
WR = CHIPS * YR
QC = NP // NY
NEAR = [(1, 0), (0, 1), (-1, 0), (0, -1), (1, 1), (-1, -1), (1, -1), (-1, 1), (2, 0), (0, 2), (2, 1), (1, 2), (2, -1), (-1, 2), (2, 2)]
DY = (2, 1, 3)


TIERS = (42, 46, 50, 56)
EARLY = (4, 10)
UNITS = 3 * 64
SR = 4


def block_of(shape, dim, first=0):
    return lax.broadcasted_iota(jnp.int32, shape, dim) // BS + first


def kernel(
    tensor, mask, group, occ, virt, out,
    xr, xl, tb, me, occ_t, vm, mv, perm, half, ys, yr, yl, cb, sb, yrs, zf, zb, zr,
    x_send, x_recv, l_send, l_recv, t_sem, y_send, y_recv, c_send, c_recv, z_send, z_recv,
):
    pa, mu = lax.axis_index("pa"), lax.axis_index("mu")
    x, z, core = pa // (2 * NZ), lax.rem(pa // 2, NZ), lax.rem(pa, 2)
    chip = x * NZ + z

    def moved(dx, dz):
        return lax.rem(x + dx + core * (dz - dx) + NX, NX), lax.rem(z + dz + core * (dx - dz) + NZ, NZ)

    def plane(x2, z2, c2):
        return ((x2 * NZ + z2) * 2 + c2, mu)

    def tensor_chunk(w):
        return pltpu.make_async_copy(tensor.at[pl.ds(w * TR, TR)], tb.at[lax.rem(w, 2)], t_sem.at[lax.rem(w, 2)])

    tensor_chunk(0).start()
    barrier = pltpu.get_barrier_semaphore()
    for c2 in (0, 1):
        for dx, dz in NEAR + [(0, 0)]:
            if (dx, dz, c2) != (0, 0, 0):
                pl.semaphore_signal(barrier, inc=1, device_id=plane(*moved(dx, dz), lax.rem(core + c2, 2)), device_id_type=MESH)
    for dy in DY:
        pl.semaphore_signal(barrier, inc=1, device_id=(pa, lax.rem(mu + dy, NY)), device_id_type=MESH)
    pl.semaphore_wait(barrier, 2 * CHIPS - 1 + NY - 1)

    def send_x(w, carry):
        def part(x2, z2, c2):
            return tensor.at[
                pl.ds(w * XR, XR),
                pl.ds(pl.multiple_of(mu * (NAO // NY) + x2 * 2 * LB + c2 * LB, LB), LB),
                pl.ds(pl.multiple_of(z2 * SB, SB), SB),
            ]

        for c2 in (0, 1):
            for dx, dz in NEAR + [(0, 0)]:
                where = (*moved(dx, dz), lax.rem(core + c2, 2))
                if (dx, dz, c2) == (0, 0, 0):
                    pltpu.make_async_copy(part(*where), xr.at[w, pa], x_recv.at[w]).start()
                else:
                    pltpu.make_async_remote_copy(
                        src_ref=part(*where), dst_ref=xr.at[w, pa], send_sem=x_send.at[w], recv_sem=x_recv.at[w],
                        device_id=plane(*where), device_id_type=MESH,
                    ).start()
        return carry

    lax.fori_loop(0, XW, send_x, 0)

    spread = (block_of((NAO, 8), 0) == lax.broadcasted_iota(jnp.int32, (NAO, 8), 1)).astype(F32)
    for g in range(3):
        blocks = mask[(ROWS * pa + 16 * g) // BS].astype(F32)
        rows = jnp.dot(spread, blocks, preferred_element_type=F32)
        me[g] = lax.dot_general(rows, spread, (((1,), (1,)), ((), ())), preferred_element_type=F32).astype(BF16)
    lane_block = lax.broadcasted_iota(jnp.int32, (8, SB), 0) == block_of((8, SB), 1, 2 * z)
    own_blocks = mask[:, pl.ds(2 * mu + x // 2, 1), :].astype(F32).reshape(NP // BS, 8)
    mv[...] = jnp.dot(own_blocks, lane_block.astype(F32), preferred_element_type=F32)
    group_row = group[...].astype(F32)
    row_group = jnp.sum(spread * group_row, axis=1, keepdims=True)
    col_group = lax.dot_general(group_row, spread, (((1,), (1,)), ((), ())), preferred_element_type=F32)
    vm[...] = jnp.where(jnp.abs(row_group - col_group) <= GROUP_REACH + 0.5, virt[...].astype(F32), 0.0).astype(BF16)
    occ_block = lax.broadcasted_iota(jnp.int32, (8, SB), 0) == block_of((8, SB), 1, 2 * mu)
    occ_group = jnp.dot(group_row, occ_block.astype(F32), preferred_element_type=F32)
    occ_cols = occ[:, pl.ds(pl.multiple_of(mu * SB, SB), SB)].astype(F32)
    occ_cols = jnp.where(jnp.abs(row_group - occ_group) <= GROUP_REACH + 0.5, occ_cols, 0.0)
    occ_t[...] = occ_cols.T.astype(BF16)
    to = lax.broadcasted_iota(jnp.int32, (256, 256), 0)
    perm[...] = (lax.broadcasted_iota(jnp.int32, (256, 256), 1) == lax.rem(to, 16) * 16 + to // 16).astype(BF16)

    def send_y(w):
        def part(x2, z2):
            return ys.at[pl.ds(w * YR, YR), pl.ds(pl.multiple_of(x2 * 2 * LB, 2 * LB), 2 * LB), pl.ds(pl.multiple_of(z2 * SB, SB), SB)]

        for dx, dz in NEAR:
            x2, z2 = moved(dx, dz)
            pltpu.make_async_remote_copy(
                src_ref=part(x2, z2), dst_ref=yr.at[w, chip], send_sem=y_send.at[w], recv_sem=y_recv.at[w],
                device_id=plane(x2, z2, core), device_id_type=MESH,
            ).start()
        pltpu.make_async_copy(part(x, z), yr.at[w, chip], y_recv.at[w]).start()

    def make_product(w, carry):
        tensor_chunk(w).wait()

        @pl.when(w + 1 < ROWS // TR)
        def _():
            tensor_chunk(w + 1).start()

        slot = lax.rem(w, 2)

        def one(p, carry):
            block = tb[slot, p] * me[w // 2]
            half[pl.ds(pl.multiple_of(p * SB, SB), SB), :] = jnp.dot(occ_t[...], block, preferred_element_type=F32).astype(BF16)
            return carry

        lax.fori_loop(0, TR, one, 0)

        def two(i, carry):
            rows = half[pl.ds(pl.multiple_of(i * 2 * SB, 2 * SB), 2 * SB), :]
            done = jnp.dot(rows, vm[...], preferred_element_type=F32).astype(BF16)
            ys[pl.ds(w * TR + 2 * i, 2)] = done.reshape(2, SB, NAO)
            return carry

        lax.fori_loop(0, TR // 2, two, 0)
        for k in range(TR // YR):
            send_y(w * (TR // YR) + k)
        return carry

    lax.fori_loop(0, ROWS // TR, make_product, 0)

    def sibling(rows, columns):
        return pltpu.make_async_remote_copy(
            src_ref=xl.at[rows, columns], dst_ref=xl.at[rows, columns], send_sem=l_send, recv_sem=l_recv,
            device_id=plane(x, z, 1 - core), device_id_type=MESH,
        )

    own = pl.multiple_of(core * KC, KC)
    other = pl.multiple_of((1 - core) * KC, KC)

    def turn(rows):
        return jnp.dot(perm[...], rows, preferred_element_type=F32).astype(BF16).reshape(16, 16, SB)

    def lay_x(w, carry):
        pltpu.make_async_copy(xr.at[w], xr.at[w], x_recv.at[w]).wait()

        def one(j, carry):
            row = pl.multiple_of(j * ROWS + w * XR, XR)
            keep = mv[pl.ds(row // BS, 1), :].astype(BF16)
            turned = turn(xr[w, j].reshape(256, SB) * keep)
            for i in range(LB):
                xl[pl.ds(row, XR), pl.ds(pl.multiple_of(own + i * SB, SB), SB)] = turned[i]
            sibling(pl.ds(row, XR), pl.ds(own, KC)).start()
            return carry

        lax.fori_loop(0, 2 * CHIPS, one, 0)
        return carry

    lax.fori_loop(0, XW, lay_x, 0)
    pltpu.make_async_copy(xl.at[:, pl.ds(other, KC)], xl.at[:, pl.ds(other, KC)], l_recv).wait()

    def partial(w, carry):
        pltpu.make_async_copy(yr.at[w], yr.at[w], y_recv.at[w]).wait()

        def lay_y(i, carry):
            for h in (0, 1):
                turned = turn(yr[w, pl.ds(16 // YR * i, 16 // YR), :, h * LB : (h + 1) * LB, :].reshape(256, SB))
                for k in range(LB):
                    yl[pl.ds(pl.multiple_of(i * 16, 16), 16), (h * LB + k) * SB : (h * LB + k + 1) * SB] = turned[k]
            return carry

        lax.fori_loop(0, WR // 16, lay_y, 0)

        def tile(y2):
            columns = xl[pl.ds(pl.multiple_of(y2 * QC, QC), QC), :]
            return lax.dot_general(yl[...], columns, (((1,), (1,)), ((), ())), preferred_element_type=F32)

        for k, dy in enumerate(DY):
            y2 = lax.rem(mu + dy, NY)
            cb[w, k] = tile(y2).astype(BF16)
            pltpu.make_async_remote_copy(
                src_ref=cb.at[w, k], dst_ref=yrs.at[w, k], send_sem=c_send.at[w], recv_sem=c_recv.at[w],
                device_id=(pa, y2), device_id_type=MESH,
            ).start()
        sb[lax.rem(w, 2)] = tile(mu)

        @pl.when(w > 0)
        def _():
            sum_y(w - 1)

        return carry

    def sum_y(w):
        pltpu.make_async_copy(yrs.at[w], yrs.at[w], c_recv.at[w]).wait()
        total = (sb[lax.rem(w, 2)] + yrs[w, 0].astype(F32)) + (yrs[w, 1].astype(F32) + yrs[w, 2].astype(F32))
        for k in range(YZ):

            @pl.when(lax.rem(w, YZ) == k)
            def _():
                zf[:, k * YR : (k + 1) * YR, :] = total.reshape(CHIPS, YR, QC)

        @pl.when(lax.rem(w, YZ) == YZ - 1)
        def _():
            send_z(w // YZ)

    def send_z(v):
        zb[v] = zf[...].astype(BF16)
        for dx, dz in NEAR:
            x2, z2 = moved(dx, dz)
            pltpu.make_async_remote_copy(
                src_ref=zb.at[v, x2 * NZ + z2], dst_ref=zr.at[v, chip], send_sem=z_send.at[v], recv_sem=z_recv.at[v],
                device_id=plane(x2, z2, core), device_id_type=MESH,
            ).start()
        pltpu.make_async_copy(zb.at[v, chip], zr.at[v, chip], z_recv.at[v]).start()

    lax.fori_loop(0, YW, partial, 0)
    sum_y(YW - 1)

    def finish(w, carry):
        pltpu.make_async_copy(zr.at[w], zr.at[w], z_recv.at[w]).wait()
        out[pl.ds(pl.multiple_of(w * ZR, ZR), ZR), :] = jnp.sum(zr[w].astype(F32), axis=0) * (1.0 / NAO)
        return carry

    lax.fori_loop(0, ZW, finish, 0)

    def left(ref, sem):
        pltpu.make_async_copy(ref, ref, sem).wait()

    left(xl.at[:, pl.ds(own, KC)], l_send)
    for w in range(XW):
        left(xr.at[w, pl.ds(0, 2 * CHIPS - 1)], x_send.at[w])
    for w in range(YW):
        left(yr.at[w, pl.ds(0, CHIPS - 1)], y_send.at[w])
        left(cb.at[w], c_send.at[w])
    for w in range(ZW):
        left(zr.at[w, pl.ds(0, CHIPS - 1)], z_send.at[w])


def whole(tensor, block_mask, group_row, green_occ, green_virt):
    vmem = pl.BlockSpec(memory_space=pltpu.VMEM)
    dma = pltpu.SemaphoreType.DMA
    return pl.pallas_call(
        kernel,
        out_shape=jax.ShapeDtypeStruct((ROWS, QC), F32),
        in_specs=[pl.BlockSpec(memory_space=pl.ANY), vmem, vmem, vmem, vmem],
        out_specs=vmem,
        scratch_shapes=[
            pltpu.VMEM((XW, 2 * CHIPS, XR, LB, SB), BF16),
            pltpu.VMEM((NP, 2 * KC), BF16),
            pltpu.VMEM((2, TR, NAO, NAO), BF16),
            pltpu.VMEM((3, NAO, NAO), BF16),
            pltpu.VMEM((SB, NAO), BF16),
            pltpu.VMEM((NAO, NAO), BF16),
            pltpu.VMEM((NP // BS, SB), F32),
            pltpu.VMEM((256, 256), BF16),
            pltpu.VMEM((TR * SB, NAO), BF16),
            pltpu.VMEM((ROWS, SB, NAO), BF16),
            pltpu.VMEM((YW, CHIPS, YR, 2 * LB, SB), BF16),
            pltpu.VMEM((WR, 2 * KC), BF16),
            pltpu.VMEM((YW, NY - 1, WR, QC), BF16),
            pltpu.VMEM((2, WR, QC), F32),
            pltpu.VMEM((YW, NY - 1, WR, QC), BF16),
            pltpu.VMEM((CHIPS, ZR, QC), F32),
            pltpu.VMEM((ZW, CHIPS, ZR, QC), BF16),
            pltpu.VMEM((ZW, CHIPS, ZR, QC), BF16),
            dma((XW,)), dma((XW,)), dma, dma, dma((2,)), dma((YW,)), dma((YW,)), dma((YW,)), dma((YW,)), dma((ZW,)), dma((ZW,)),
        ],
        compiler_params=pltpu.CompilerParams(collective_id=0, has_side_effects=True, vmem_limit_bytes=60 * 2**20),
    )(tensor, block_mask, group_row, green_occ, green_virt)


def granule_rows(chip, core):
    odd = lax.rem(chip, 2)
    gives = 2 - odd - core
    first = jnp.where(gives == 0, 1, 0)
    second = jnp.where(gives == 2, 1, 2)
    row = chip * (2 * ROWS)
    return row + core * ROWS + first * 16, row + core * ROWS + second * 16, row + (4 - 2 * core - odd) * 16, row + core * ROWS + gives * 16


def slot_waves(slots):
    late = slots - sum(EARLY)
    third = late // 4 * 2
    return *EARLY, third, late - third


def dot(a, b):
    return jnp.dot(a, b, preferred_element_type=F32)


def iota(shape, dim):
    return lax.broadcasted_iota(jnp.int32, shape, dim)


def packed_kernel(
    slots,
    tensor, mask, group, occ, virt, out,
    xa, xb, xs, xr, xl, tb, me, occ_f, occ_t, vm, perms, sel, tabs, own_pos, half, ys, yr, yl, cb, sb, yrs, zf, zb, zr, spots,
    i_sem, e_send, e_recv, x_send, x_recv, l_send, l_recv, t_sem, y_send, y_recv, c_send, c_recv, z_send, z_recv, s_sem,
):
    pa, mu = lax.axis_index("pa"), lax.axis_index("mu")
    x, z, core = pa // (2 * NZ), lax.rem(pa // 2, NZ), lax.rem(pa, 2)
    chip = x * NZ + z

    def moved(dx, dz):
        return lax.rem(x + dx + core * (dz - dx) + NX, NX), lax.rem(z + dz + core * (dx - dz) + NZ, NZ)

    def plane(x2, z2, c2):
        return ((x2 * NZ + z2) * 2 + c2, mu)

    def wait(ref, sem):
        pltpu.make_async_copy(ref, ref, sem).wait()

    def to_chips(source, target, send, recv):
        for dx, dz in NEAR:
            x2, z2 = moved(dx, dz)
            pltpu.make_async_remote_copy(
                src_ref=source(x2 * NZ + z2), dst_ref=target, send_sem=send, recv_sem=recv,
                device_id=plane(x2, z2, core), device_id_type=MESH,
            ).start()
        pltpu.make_async_copy(source(chip), target, recv).start()

    def tensor_chunk(w):
        return pltpu.make_async_copy(tensor.at[pl.ds(w * SR, SR)], tb.at[lax.rem(w, 2)], t_sem.at[lax.rem(w, 2)])

    own_rows = granule_rows(chip, core)

    def x_block(granule, v):
        a, b = v // 4, lax.rem(v, 4)
        row = pl.multiple_of(own_rows[granule] - pa * ROWS, 16)
        return tensor.at[pl.ds(row, 16), pl.ds(pl.multiple_of(a * BS + mu * LB, LB), LB), pl.ds(pl.multiple_of(b * SB, SB), SB)]

    def load_x(v, carry):
        for g in (0, 1):
            pltpu.make_async_copy(x_block(g, v), xa.at[g * 32 + v], i_sem).start()
        return carry

    lax.fori_loop(0, 32, load_x, 0)
    tensor_chunk(0).start()
    barrier = pltpu.get_barrier_semaphore()
    for dx, dz in NEAR:
        pl.semaphore_signal(barrier, inc=1, device_id=plane(*moved(dx, dz), core), device_id_type=MESH)
    pl.semaphore_signal(barrier, inc=1, device_id=plane(x, z, 1 - core), device_id_type=MESH)
    for dy in DY:
        pl.semaphore_signal(barrier, inc=1, device_id=(pa, lax.rem(mu + dy, NY)), device_id_type=MESH)
    pl.semaphore_wait(barrier, CHIPS + NY - 1)

    def give_x(v, carry):
        pltpu.make_async_remote_copy(
            src_ref=x_block(3, v), dst_ref=xb.at[v], send_sem=e_send, recv_sem=e_recv,
            device_id=plane(x, z, 1 - core), device_id_type=MESH,
        ).start()
        return carry

    lax.fori_loop(0, 32, give_x, 0)

    sizes = slot_waves(slots)
    starts = [sum(sizes[:w]) for w in range(len(sizes))]

    by_block = mask[...].astype(F32).reshape(64, NP // BS).astype(BF16)
    kept = jnp.zeros((2 * CHIPS, 256), F32)
    for g in range(3):
        device = iota((2 * CHIPS, NP // BS), 0)
        first_row = granule_rows(device // 2, lax.rem(device, 2))[g]
        rows = (first_row // BS == iota((2 * CHIPS, NP // BS), 1)).astype(F32).astype(BF16)
        units = lax.dot_general(rows, by_block, (((1,), (1,)), ((), ())), preferred_element_type=F32).astype(BF16)
        place = (iota((64, 256), 1) == iota((64, 256), 0) + 64 * g).astype(F32).astype(BF16)
        kept += dot(units, place)
    upto = (iota((256, 256), 0) <= iota((256, 256), 1)).astype(F32).astype(BF16)
    place_of = dot(kept.astype(BF16), upto)
    ours = jnp.sum(jnp.where(iota((2 * CHIPS, 256), 1) < 128, kept, 0.0), axis=1, keepdims=True)
    place_of += jnp.where(iota((2 * CHIPS, 256), 1) < 128, 0.0, jnp.maximum(2 * sum(EARLY) - ours, 0.0))
    own_pos[...] = place_of * kept
    order = place_of.astype(jnp.int32) - 1
    odd = lax.rem(iota((2 * CHIPS, 256), 1), 2)
    spot = order // 2 + jnp.where(lax.rem(order + 2, 2) == odd, 0, slots)
    tabs[0 : 2 * CHIPS] = jnp.clip(jnp.where(kept > 0.5, spot, 2 * slots), 0, 2 * slots)
    taken = (own_pos[pl.ds(pa, 1), :] == (iota((256, 256), 0) + 1).astype(F32)).astype(F32).astype(BF16)
    units = iota((8, 256), 1).astype(F32).astype(BF16)
    unit = lax.dot_general(units, taken, (((1,), (1,)), ((), ())), preferred_element_type=F32).astype(jnp.int32)
    there = lax.dot_general(jnp.ones((8, 256), BF16), taken, (((1,), (1,)), ((), ())), preferred_element_type=F32).astype(jnp.int32)
    tabs[2 * CHIPS : 2 * CHIPS + 8] = jnp.clip(unit // 2, 0, 63)
    tabs[2 * CHIPS + 16 : 2 * CHIPS + 24] = unit // 128
    tabs[2 * CHIPS + 24 : 2 * CHIPS + 32] = jnp.clip(unit // 2 - 64, 0, 31)
    tabs[2 * CHIPS + 8 : 2 * CHIPS + 16] = jnp.clip(there * (1 + lax.rem(unit, 2)), 0, 2)
    to_smem = pltpu.make_async_copy(tabs, spots, s_sem)
    to_smem.start()

    to, at = iota((256, 256), 0), iota((256, 256), 1)
    perms[0] = (at == lax.rem(to, 16) * 16 + to // 16).astype(BF16)
    perms[1] = (at == (lax.rem(to, 8) * 2 + lax.rem(to // 8, 2)) * 16 + to // 16).astype(BF16)
    perms[2] = (at == lax.rem(to, 128) // 8 * 16 + to // 128 * 8 + lax.rem(to, 8)).astype(BF16)
    frm, into = iota((SB, SB), 0), iota((SB, SB), 1)
    for h in (0, 1):
        sel[0, h] = jnp.zeros((SB, SB), BF16)
        for b in (0, 1):
            sel[1 + b, h] = ((frm - BS * b == into - BS * h) & (into // BS == h)).astype(BF16)
    sel[3, 0] = (lax.rem(frm + BS, SB) == into).astype(BF16)

    to_smem.wait()
    wait(xa, i_sem)

    for w, n in enumerate(sizes):
        if w == len(EARLY):
            wait(xb, e_recv)

        def one(i, carry):
            for k in range(2):
                r = starts[w] + i * 2 + k
                full = jnp.zeros((256, SB), F32)
                for h in (0, 1):
                    cube = xa[spots[2 * CHIPS, 2 * r + h]]
                    if w >= len(EARLY):
                        cube = jnp.where(spots[2 * CHIPS + 16, 2 * r + h] > 0, xb[spots[2 * CHIPS + 24, 2 * r + h]], cube)
                    cube = cube.reshape(256, SB)
                    full += dot(cube, sel[spots[2 * CHIPS + 8, 2 * r + h], h])
                xs[:, r] = dot(perms[0], full.astype(BF16)).astype(BF16).reshape(16, 16, SB)
            return carry

        lax.fori_loop(0, n // 2, one, 0)
        part = pl.ds(starts[w], n)
        to_chips(lambda t: xs.at[t, part], xr.at[chip, part], x_send.at[w], x_recv.at[w])

    spread = (block_of((NAO, 8), 0) == iota((NAO, 8), 1)).astype(F32)
    for g in range(3):
        this = iota((8, 8, NP // BS), 2) == (ROWS * pa + 16 * g) // BS
        rows = dot(spread, jnp.sum(jnp.where(this, mask[...].astype(F32), 0.0), axis=2))
        me[g] = lax.dot_general(rows, spread, (((1,), (1,)), ((), ())), preferred_element_type=F32).astype(BF16)
    group_row = group[...].astype(F32)
    row_group = jnp.sum(spread * group_row, axis=1, keepdims=True)
    col_group = lax.dot_general(group_row, spread, (((1,), (1,)), ((), ())), preferred_element_type=F32)
    near = jnp.abs(row_group - col_group) <= GROUP_REACH + 0.5
    vm[...] = jnp.where(near, virt[...].astype(F32), 0.0).astype(BF16)
    occ_f[...] = jnp.where(near, occ[...].astype(F32), 0.0).T
    for a in range(8):
        occ_t[a * LB : (a + 1) * LB] = occ_f[pl.ds(pl.multiple_of(a * BS + mu * LB, LB), LB), :].astype(BF16)

    def make_product(w, carry):
        for part in range(YR // SR):
            v = w * (YR // SR) + part
            tensor_chunk(v).wait()

            @pl.when(v + 1 < ROWS // SR)
            def _():
                tensor_chunk(v + 1).start()

            def one(p, carry):
                block = tb[lax.rem(v, 2), p] * me[w // 2]
                half[part * SR + p] = dot(occ_t[...], block).astype(BF16)
                return carry

            lax.fori_loop(0, SR, one, 0)
        for a in range(4):
            done = dot(half[:, a * 2 * LB : (a + 1) * 2 * LB, :].reshape(256, NAO), vm[...]).astype(BF16)
            ys[w, :, :, a * NAO : (a + 1) * NAO] = dot(perms[1], done).astype(BF16).reshape(16, 16, NAO)
        to_chips(lambda t: ys.at[w, t], yr.at[w, chip], y_send.at[w], y_recv.at[w])
        return carry

    lax.fori_loop(0, YW, make_product, 0)

    for w, n in enumerate(sizes):
        wait(xr.at[:, pl.ds(starts[w], n)], x_recv.at[w])
    left_half = iota((16, SB), 1) < BS

    def unpack(i, carry):
        rows = dot(xr[i, 0:slots].reshape(slots * 16, SB), sel[3, 0])
        xr[i, slots : 2 * slots] = rows.astype(BF16).reshape(slots, 16, SB)
        xr[i, 2 * slots] = jnp.zeros((16, SB), BF16)
        j = 2 * i + core
        for g in range(3):
            row = pl.multiple_of(granule_rows(i, core)[g], 16)
            for a in range(8):
                for b in range(4):
                    u = (g * 8 + a) * 8 + 2 * b
                    both = jnp.where(left_half, xr[i, spots[j, u]], xr[i, spots[j, u + 1]])
                    first = a % 2 * KC + a // 2 * NAO + b * SB
                    xl[pl.ds(row, 16), first : first + SB] = both
            rows = pl.ds(row, 16)
            pltpu.make_async_remote_copy(
                src_ref=xl.at[rows], dst_ref=xl.at[rows], send_sem=l_send, recv_sem=l_recv,
                device_id=plane(x, z, 1 - core), device_id_type=MESH,
            ).start()
        return carry

    lax.fori_loop(0, CHIPS, unpack, 0)
    wait(xl.at[pl.ds(0, NP // 2)], l_recv)

    def partial(w, carry):
        wait(yr.at[w], y_recv.at[w])
        for k in range(4):
            rows = yr[w, :, :, k * NAO : (k + 1) * NAO].reshape(256, NAO)
            turned = dot(perms[2], rows).astype(BF16)
            yl[:, k * NAO : (k + 1) * NAO] = turned[:WR]
            yl[:, KC + k * NAO : KC + (k + 1) * NAO] = turned[WR:]

        def tile(y2):
            columns = xl[pl.ds(pl.multiple_of(y2 * QC, QC), QC), :]
            return lax.dot_general(yl[...], columns, (((1,), (1,)), ((), ())), preferred_element_type=F32)

        for k, dy in enumerate(DY):
            y2 = lax.rem(mu + dy, NY)
            cb[w, k] = tile(y2).astype(BF16)
            pltpu.make_async_remote_copy(
                src_ref=cb.at[w, k], dst_ref=yrs.at[w, k], send_sem=c_send.at[w], recv_sem=c_recv.at[w],
                device_id=(pa, y2), device_id_type=MESH,
            ).start()
        sb[lax.rem(w, 2)] = tile(mu)

        @pl.when(w > 0)
        def _():
            sum_y(w - 1)

        return carry

    def sum_y(w):
        wait(yrs.at[w], c_recv.at[w])
        total = (sb[lax.rem(w, 2)] + yrs[w, 0].astype(F32)) + (yrs[w, 1].astype(F32) + yrs[w, 2].astype(F32))
        for k in range(YZ):

            @pl.when(lax.rem(w, YZ) == k)
            def _():
                zf[:, k * YR : (k + 1) * YR, :] = total.reshape(CHIPS, YR, QC)

        @pl.when(lax.rem(w, YZ) == YZ - 1)
        def _():
            v = w // YZ
            zb[v] = zf[...].astype(BF16)
            to_chips(lambda t: zb.at[v, t], zr.at[v, chip], z_send.at[v], z_recv.at[v])

    lax.fori_loop(0, YW, partial, 0)
    sum_y(YW - 1)

    def finish(w, carry):
        wait(zr.at[w], z_recv.at[w])
        out[pl.ds(pl.multiple_of(w * ZR, ZR), ZR), :] = jnp.sum(zr[w].astype(F32), axis=0) * (1.0 / NAO)
        return carry

    lax.fori_loop(0, ZW, finish, 0)

    wait(xb, e_send)
    wait(xl.at[pl.ds(0, NP // 2)], l_send)
    for w, n in enumerate(sizes):
        wait(xs.at[pl.ds(0, CHIPS - 1), pl.ds(0, n)], x_send.at[w])
    for w in range(YW):
        wait(yr.at[w, pl.ds(0, CHIPS - 1)], y_send.at[w])
        wait(cb.at[w], c_send.at[w])
    for w in range(ZW):
        wait(zr.at[w, pl.ds(0, CHIPS - 1)], z_send.at[w])


def packed(tier, tensor, block_mask, group_row, green_occ, green_virt):
    slots = TIERS[tier]
    waves = len(slot_waves(slots))
    vmem = pl.BlockSpec(memory_space=pltpu.VMEM)
    dma = pltpu.SemaphoreType.DMA
    return pl.pallas_call(
        functools.partial(packed_kernel, slots),
        out_shape=jax.ShapeDtypeStruct((ROWS, QC), F32),
        in_specs=[pl.BlockSpec(memory_space=pl.ANY), vmem, vmem, vmem, vmem],
        out_specs=vmem,
        scratch_shapes=[
            pltpu.VMEM((64, 16, LB, SB), BF16),
            pltpu.VMEM((32, 16, LB, SB), BF16),
            pltpu.VMEM((CHIPS, slots, 16, SB), BF16),
            pltpu.VMEM((CHIPS, 2 * slots + 1, 16, SB), BF16),
            pltpu.VMEM((NP, 2 * KC), BF16),
            pltpu.VMEM((2, SR, NAO, NAO), BF16),
            pltpu.VMEM((3, NAO, NAO), BF16),
            pltpu.VMEM((NAO, NAO), F32),
            pltpu.VMEM((SB, NAO), BF16),
            pltpu.VMEM((NAO, NAO), BF16),
            pltpu.VMEM((3, 256, 256), BF16),
            pltpu.VMEM((4, 2, SB, SB), BF16),
            pltpu.VMEM((2 * CHIPS + 32, 256), jnp.int32),
            pltpu.VMEM((2 * CHIPS, 256), F32),
            pltpu.VMEM((YR, SB, NAO), BF16),
            pltpu.VMEM((YW, CHIPS, 16, KC), BF16),
            pltpu.VMEM((YW, CHIPS, 16, KC), BF16),
            pltpu.VMEM((WR, 2 * KC), BF16),
            pltpu.VMEM((YW, NY - 1, WR, QC), BF16),
            pltpu.VMEM((2, WR, QC), F32),
            pltpu.VMEM((YW, NY - 1, WR, QC), BF16),
            pltpu.VMEM((CHIPS, ZR, QC), F32),
            pltpu.VMEM((ZW, CHIPS, ZR, QC), BF16),
            pltpu.VMEM((ZW, CHIPS, ZR, QC), BF16),
            pltpu.SMEM((2 * CHIPS + 32, 256), jnp.int32),
            dma, dma, dma, dma((waves,)), dma((waves,)), dma, dma, dma((2,)), dma((YW,)), dma((YW,)), dma((YW,)), dma((YW,)), dma((ZW,)), dma((ZW,)), dma,
        ],
        compiler_params=pltpu.CompilerParams(collective_id=1 + tier, has_side_effects=True, vmem_limit_bytes=62 * 2**20),
    )(tensor, jnp.transpose(block_mask, (1, 2, 0)), group_row, green_occ, green_virt)


def shards(tensor, block_mask, group_of_block, green_occ, green_virt):
    kept = jnp.sum(block_mask, axis=(1, 2)).reshape(NP // BS // 3, 3)
    a, b, c = kept[:, 0], kept[:, 1], kept[:, 2]
    most = 0
    for keeps, gets in ((2 * a, b), (a + b, a), (b + c, c), (2 * c, b)):
        most = jnp.maximum(most, jnp.maximum(keeps, 2 * sum(EARLY)) + gets)
    branches = [functools.partial(packed, tier) for tier in range(len(TIERS))] + [whole]
    which = jnp.max(sum((most > 2 * slots).astype(jnp.int32) for slots in TIERS))
    return lax.switch(which, branches, tensor, block_mask, group_of_block.reshape(1, 8), green_occ, green_virt)


def solution(mesh):
    placed = (P("pa", None, None), P(), P(), P(), P())
    return jax.shard_map(shards, mesh=mesh, in_specs=placed, out_specs=P("pa", "mu"), check_vma=False)
```

```python
import functools

import jax
import jax.numpy as jnp
from jax import lax
from jax.experimental import pallas as pl
from jax.experimental.pallas import tpu as pltpu
from jax.sharding import PartitionSpec as P

MESH = pl.DeviceIdType.MESH
F32, BF16 = jnp.float32, jnp.bfloat16

BS = 64
GROUP_REACH = 1
NX = NZ = NY = 4
CHIPS = NX * NZ
ROWS = 48
NP = 1536
NAO = 512
LB = 16
SB = 128
KC = LB * SB
XW = 3
XR = ROWS // XW
YW = 6
YR = ROWS // YW
TR = 8
ZW = 3
ZR = ROWS // ZW
YZ = ZR // YR
WR = CHIPS * YR
QC = NP // NY
NEAR = [(1, 0), (0, 1), (-1, 0), (0, -1), (1, 1), (-1, -1), (1, -1), (-1, 1), (2, 0), (0, 2), (2, 1), (1, 2), (2, -1), (-1, 2), (2, 2)]
DY = (2, 1, 3)


TIERS = (42, 46, 50, 56)
EARLY = (4, 10)
UNITS = 3 * 64
SR = 4


def block_of(shape, dim, first=0):
    return lax.broadcasted_iota(jnp.int32, shape, dim) // BS + first


def kernel(
    tensor, mask, group, occ, virt, out,
    xr, xl, tb, me, occ_t, vm, mv, perm, half, ys, yr, yl, cb, sb, yrs, zf, zb, zr,
    x_send, x_recv, l_send, l_recv, t_sem, y_send, y_recv, c_send, c_recv, z_send, z_recv,
):
    pa, mu = lax.axis_index("pa"), lax.axis_index("mu")
    x, z, core = pa // (2 * NZ), lax.rem(pa // 2, NZ), lax.rem(pa, 2)
    chip = x * NZ + z

    def moved(dx, dz):
        return lax.rem(x + dx + core * (dz - dx) + NX, NX), lax.rem(z + dz + core * (dx - dz) + NZ, NZ)

    def plane(x2, z2, c2):
        return ((x2 * NZ + z2) * 2 + c2, mu)

    def tensor_chunk(w):
        return pltpu.make_async_copy(tensor.at[pl.ds(w * TR, TR)], tb.at[lax.rem(w, 2)], t_sem.at[lax.rem(w, 2)])

    tensor_chunk(0).start()
    barrier = pltpu.get_barrier_semaphore()
    for c2 in (0, 1):
        for dx, dz in NEAR + [(0, 0)]:
            if (dx, dz, c2) != (0, 0, 0):
                pl.semaphore_signal(barrier, inc=1, device_id=plane(*moved(dx, dz), lax.rem(core + c2, 2)), device_id_type=MESH)
    for dy in DY:
        pl.semaphore_signal(barrier, inc=1, device_id=(pa, lax.rem(mu + dy, NY)), device_id_type=MESH)
    pl.semaphore_wait(barrier, 2 * CHIPS - 1 + NY - 1)

    def send_x(w, carry):
        def part(x2, z2, c2):
            return tensor.at[
                pl.ds(w * XR, XR),
                pl.ds(pl.multiple_of(mu * (NAO // NY) + x2 * 2 * LB + c2 * LB, LB), LB),
                pl.ds(pl.multiple_of(z2 * SB, SB), SB),
            ]

        for c2 in (0, 1):
            for dx, dz in NEAR + [(0, 0)]:
                where = (*moved(dx, dz), lax.rem(core + c2, 2))
                if (dx, dz, c2) == (0, 0, 0):
                    pltpu.make_async_copy(part(*where), xr.at[w, pa], x_recv.at[w]).start()
                else:
                    pltpu.make_async_remote_copy(
                        src_ref=part(*where), dst_ref=xr.at[w, pa], send_sem=x_send.at[w], recv_sem=x_recv.at[w],
                        device_id=plane(*where), device_id_type=MESH,
                    ).start()
        return carry

    lax.fori_loop(0, XW, send_x, 0)

    spread = (block_of((NAO, 8), 0) == lax.broadcasted_iota(jnp.int32, (NAO, 8), 1)).astype(F32)
    for g in range(3):
        blocks = mask[(ROWS * pa + 16 * g) // BS].astype(F32)
        rows = jnp.dot(spread, blocks, preferred_element_type=F32)
        me[g] = lax.dot_general(rows, spread, (((1,), (1,)), ((), ())), preferred_element_type=F32).astype(BF16)
    lane_block = lax.broadcasted_iota(jnp.int32, (8, SB), 0) == block_of((8, SB), 1, 2 * z)
    own_blocks = mask[:, pl.ds(2 * mu + x // 2, 1), :].astype(F32).reshape(NP // BS, 8)
    mv[...] = jnp.dot(own_blocks, lane_block.astype(F32), preferred_element_type=F32)
    group_row = group[...].astype(F32)
    row_group = jnp.sum(spread * group_row, axis=1, keepdims=True)
    col_group = lax.dot_general(group_row, spread, (((1,), (1,)), ((), ())), preferred_element_type=F32)
    vm[...] = jnp.where(jnp.abs(row_group - col_group) <= GROUP_REACH + 0.5, virt[...].astype(F32), 0.0).astype(BF16)
    occ_block = lax.broadcasted_iota(jnp.int32, (8, SB), 0) == block_of((8, SB), 1, 2 * mu)
    occ_group = jnp.dot(group_row, occ_block.astype(F32), preferred_element_type=F32)
    occ_cols = occ[:, pl.ds(pl.multiple_of(mu * SB, SB), SB)].astype(F32)
    occ_cols = jnp.where(jnp.abs(row_group - occ_group) <= GROUP_REACH + 0.5, occ_cols, 0.0)
    occ_t[...] = occ_cols.T.astype(BF16)
    to = lax.broadcasted_iota(jnp.int32, (256, 256), 0)
    perm[...] = (lax.broadcasted_iota(jnp.int32, (256, 256), 1) == lax.rem(to, 16) * 16 + to // 16).astype(BF16)

    def send_y(w):
        def part(x2, z2):
            return ys.at[pl.ds(w * YR, YR), pl.ds(pl.multiple_of(x2 * 2 * LB, 2 * LB), 2 * LB), pl.ds(pl.multiple_of(z2 * SB, SB), SB)]

        for dx, dz in NEAR:
            x2, z2 = moved(dx, dz)
            pltpu.make_async_remote_copy(
                src_ref=part(x2, z2), dst_ref=yr.at[w, chip], send_sem=y_send.at[w], recv_sem=y_recv.at[w],
                device_id=plane(x2, z2, core), device_id_type=MESH,
            ).start()
        pltpu.make_async_copy(part(x, z), yr.at[w, chip], y_recv.at[w]).start()

    def make_product(w, carry):
        tensor_chunk(w).wait()

        @pl.when(w + 1 < ROWS // TR)
        def _():
            tensor_chunk(w + 1).start()

        slot = lax.rem(w, 2)

        def one(p, carry):
            block = tb[slot, p] * me[w // 2]
            half[pl.ds(pl.multiple_of(p * SB, SB), SB), :] = jnp.dot(occ_t[...], block, preferred_element_type=F32).astype(BF16)
            return carry

        lax.fori_loop(0, TR, one, 0)

        def two(i, carry):
            rows = half[pl.ds(pl.multiple_of(i * 2 * SB, 2 * SB), 2 * SB), :]
            done = jnp.dot(rows, vm[...], preferred_element_type=F32).astype(BF16)
            ys[pl.ds(w * TR + 2 * i, 2)] = done.reshape(2, SB, NAO)
            return carry

        lax.fori_loop(0, TR // 2, two, 0)
        for k in range(TR // YR):
            send_y(w * (TR // YR) + k)
        return carry

    lax.fori_loop(0, ROWS // TR, make_product, 0)

    def sibling(rows, columns):
        return pltpu.make_async_remote_copy(
            src_ref=xl.at[rows, columns], dst_ref=xl.at[rows, columns], send_sem=l_send, recv_sem=l_recv,
            device_id=plane(x, z, 1 - core), device_id_type=MESH,
        )

    own = pl.multiple_of(core * KC, KC)
    other = pl.multiple_of((1 - core) * KC, KC)

    def turn(rows):
        return jnp.dot(perm[...], rows, preferred_element_type=F32).astype(BF16).reshape(16, 16, SB)

    def lay_x(w, carry):
        pltpu.make_async_copy(xr.at[w], xr.at[w], x_recv.at[w]).wait()

        def one(j, carry):
            row = pl.multiple_of(j * ROWS + w * XR, XR)
            keep = mv[pl.ds(row // BS, 1), :].astype(BF16)
            turned = turn(xr[w, j].reshape(256, SB) * keep)
            for i in range(LB):
                xl[pl.ds(row, XR), pl.ds(pl.multiple_of(own + i * SB, SB), SB)] = turned[i]
            sibling(pl.ds(row, XR), pl.ds(own, KC)).start()
            return carry

        lax.fori_loop(0, 2 * CHIPS, one, 0)
        return carry

    lax.fori_loop(0, XW, lay_x, 0)
    pltpu.make_async_copy(xl.at[:, pl.ds(other, KC)], xl.at[:, pl.ds(other, KC)], l_recv).wait()

    def partial(w, carry):
        pltpu.make_async_copy(yr.at[w], yr.at[w], y_recv.at[w]).wait()

        def lay_y(i, carry):
            for h in (0, 1):
                turned = turn(yr[w, pl.ds(16 // YR * i, 16 // YR), :, h * LB : (h + 1) * LB, :].reshape(256, SB))
                for k in range(LB):
                    yl[pl.ds(pl.multiple_of(i * 16, 16), 16), (h * LB + k) * SB : (h * LB + k + 1) * SB] = turned[k]
            return carry

        lax.fori_loop(0, WR // 16, lay_y, 0)

        def tile(y2):
            columns = xl[pl.ds(pl.multiple_of(y2 * QC, QC), QC), :]
            return lax.dot_general(yl[...], columns, (((1,), (1,)), ((), ())), preferred_element_type=F32)

        for k, dy in enumerate(DY):
            y2 = lax.rem(mu + dy, NY)
            cb[w, k] = tile(y2).astype(BF16)
            pltpu.make_async_remote_copy(
                src_ref=cb.at[w, k], dst_ref=yrs.at[w, k], send_sem=c_send.at[w], recv_sem=c_recv.at[w],
                device_id=(pa, y2), device_id_type=MESH,
            ).start()
        sb[lax.rem(w, 2)] = tile(mu)

        @pl.when(w > 0)
        def _():
            sum_y(w - 1)

        return carry

    def sum_y(w):
        pltpu.make_async_copy(yrs.at[w], yrs.at[w], c_recv.at[w]).wait()
        total = (sb[lax.rem(w, 2)] + yrs[w, 0].astype(F32)) + (yrs[w, 1].astype(F32) + yrs[w, 2].astype(F32))
        for k in range(YZ):

            @pl.when(lax.rem(w, YZ) == k)
            def _():
                zf[:, k * YR : (k + 1) * YR, :] = total.reshape(CHIPS, YR, QC)

        @pl.when(lax.rem(w, YZ) == YZ - 1)
        def _():
            send_z(w // YZ)

    def send_z(v):
        zb[v] = zf[...].astype(BF16)
        for dx, dz in NEAR:
            x2, z2 = moved(dx, dz)
            pltpu.make_async_remote_copy(
                src_ref=zb.at[v, x2 * NZ + z2], dst_ref=zr.at[v, chip], send_sem=z_send.at[v], recv_sem=z_recv.at[v],
                device_id=plane(x2, z2, core), device_id_type=MESH,
            ).start()
        pltpu.make_async_copy(zb.at[v, chip], zr.at[v, chip], z_recv.at[v]).start()

    lax.fori_loop(0, YW, partial, 0)
    sum_y(YW - 1)

    def finish(w, carry):
        pltpu.make_async_copy(zr.at[w], zr.at[w], z_recv.at[w]).wait()
        out[pl.ds(pl.multiple_of(w * ZR, ZR), ZR), :] = jnp.sum(zr[w].astype(F32), axis=0) * (1.0 / NAO)
        return carry

    lax.fori_loop(0, ZW, finish, 0)

    def left(ref, sem):
        pltpu.make_async_copy(ref, ref, sem).wait()

    left(xl.at[:, pl.ds(own, KC)], l_send)
    for w in range(XW):
        left(xr.at[w, pl.ds(0, 2 * CHIPS - 1)], x_send.at[w])
    for w in range(YW):
        left(yr.at[w, pl.ds(0, CHIPS - 1)], y_send.at[w])
        left(cb.at[w], c_send.at[w])
    for w in range(ZW):
        left(zr.at[w, pl.ds(0, CHIPS - 1)], z_send.at[w])


def whole(tensor, block_mask, group_row, green_occ, green_virt):
    vmem = pl.BlockSpec(memory_space=pltpu.VMEM)
    dma = pltpu.SemaphoreType.DMA
    return pl.pallas_call(
        kernel,
        out_shape=jax.ShapeDtypeStruct((ROWS, QC), F32),
        in_specs=[pl.BlockSpec(memory_space=pl.ANY), vmem, vmem, vmem, vmem],
        out_specs=vmem,
        scratch_shapes=[
            pltpu.VMEM((XW, 2 * CHIPS, XR, LB, SB), BF16),
            pltpu.VMEM((NP, 2 * KC), BF16),
            pltpu.VMEM((2, TR, NAO, NAO), BF16),
            pltpu.VMEM((3, NAO, NAO), BF16),
            pltpu.VMEM((SB, NAO), BF16),
            pltpu.VMEM((NAO, NAO), BF16),
            pltpu.VMEM((NP // BS, SB), F32),
            pltpu.VMEM((256, 256), BF16),
            pltpu.VMEM((TR * SB, NAO), BF16),
            pltpu.VMEM((ROWS, SB, NAO), BF16),
            pltpu.VMEM((YW, CHIPS, YR, 2 * LB, SB), BF16),
            pltpu.VMEM((WR, 2 * KC), BF16),
            pltpu.VMEM((YW, NY - 1, WR, QC), BF16),
            pltpu.VMEM((2, WR, QC), F32),
            pltpu.VMEM((YW, NY - 1, WR, QC), BF16),
            pltpu.VMEM((CHIPS, ZR, QC), F32),
            pltpu.VMEM((ZW, CHIPS, ZR, QC), BF16),
            pltpu.VMEM((ZW, CHIPS, ZR, QC), BF16),
            dma((XW,)), dma((XW,)), dma, dma, dma((2,)), dma((YW,)), dma((YW,)), dma((YW,)), dma((YW,)), dma((ZW,)), dma((ZW,)),
        ],
        compiler_params=pltpu.CompilerParams(collective_id=0, has_side_effects=True, vmem_limit_bytes=60 * 2**20),
    )(tensor, block_mask, group_row, green_occ, green_virt)


def granule_rows(chip, core):
    odd = lax.rem(chip, 2)
    gives = 2 - odd - core
    first = jnp.where(gives == 0, 1, 0)
    second = jnp.where(gives == 2, 1, 2)
    row = chip * (2 * ROWS)
    return row + core * ROWS + first * 16, row + core * ROWS + second * 16, row + (4 - 2 * core - odd) * 16, row + core * ROWS + gives * 16


def slot_waves(slots):
    late = slots - sum(EARLY)
    third = late // 4 * 2
    return *EARLY, third, late - third


def dot(a, b):
    return jnp.dot(a, b, preferred_element_type=F32)


def iota(shape, dim):
    return lax.broadcasted_iota(jnp.int32, shape, dim)


def packed_kernel(
    slots,
    tensor, mask, group, occ, virt, out,
    xa, xb, xs, xr, xl, tb, me, occ_f, occ_t, vm, perms, sel, tabs, own_pos, half, ys, yr, yl, cb, sb, yrs, zf, zb, zr, spots,
    i_sem, e_send, e_recv, x_send, x_recv, l_send, l_recv, t_sem, y_send, y_recv, c_send, c_recv, z_send, z_recv, s_sem,
):
    pa, mu = lax.axis_index("pa"), lax.axis_index("mu")
    x, z, core = pa // (2 * NZ), lax.rem(pa // 2, NZ), lax.rem(pa, 2)
    chip = x * NZ + z

    def moved(dx, dz):
        return lax.rem(x + dx + core * (dz - dx) + NX, NX), lax.rem(z + dz + core * (dx - dz) + NZ, NZ)

    def plane(x2, z2, c2):
        return ((x2 * NZ + z2) * 2 + c2, mu)

    def wait(ref, sem):
        pltpu.make_async_copy(ref, ref, sem).wait()

    def to_chips(source, target, send, recv):
        for dx, dz in NEAR:
            x2, z2 = moved(dx, dz)
            pltpu.make_async_remote_copy(
                src_ref=source(x2 * NZ + z2), dst_ref=target, send_sem=send, recv_sem=recv,
                device_id=plane(x2, z2, core), device_id_type=MESH,
            ).start()
        pltpu.make_async_copy(source(chip), target, recv).start()

    def tensor_chunk(w):
        return pltpu.make_async_copy(tensor.at[pl.ds(w * SR, SR)], tb.at[lax.rem(w, 2)], t_sem.at[lax.rem(w, 2)])

    own_rows = granule_rows(chip, core)

    def x_block(granule, v):
        a, b = v // 4, lax.rem(v, 4)
        row = pl.multiple_of(own_rows[granule] - pa * ROWS, 16)
        return tensor.at[pl.ds(row, 16), pl.ds(pl.multiple_of(a * BS + mu * LB, LB), LB), pl.ds(pl.multiple_of(b * SB, SB), SB)]

    def load_x(v, carry):
        for g in (0, 1):
            pltpu.make_async_copy(x_block(g, v), xa.at[g * 32 + v], i_sem).start()
        return carry

    lax.fori_loop(0, 32, load_x, 0)
    tensor_chunk(0).start()
    barrier = pltpu.get_barrier_semaphore()
    for dx, dz in NEAR:
        pl.semaphore_signal(barrier, inc=1, device_id=plane(*moved(dx, dz), core), device_id_type=MESH)
    pl.semaphore_signal(barrier, inc=1, device_id=plane(x, z, 1 - core), device_id_type=MESH)
    for dy in DY:
        pl.semaphore_signal(barrier, inc=1, device_id=(pa, lax.rem(mu + dy, NY)), device_id_type=MESH)

    sizes = slot_waves(slots)
    starts = [sum(sizes[:w]) for w in range(len(sizes))]

    by_block = mask[...].astype(F32).reshape(64, NP // BS).astype(BF16)
    kept = jnp.zeros((2 * CHIPS, 256), F32)
    for g in range(3):
        device = iota((2 * CHIPS, NP // BS), 0)
        first_row = granule_rows(device // 2, lax.rem(device, 2))[g]
        rows = (first_row // BS == iota((2 * CHIPS, NP // BS), 1)).astype(F32).astype(BF16)
        units = lax.dot_general(rows, by_block, (((1,), (1,)), ((), ())), preferred_element_type=F32).astype(BF16)
        place = (iota((64, 256), 1) == iota((64, 256), 0) + 64 * g).astype(F32).astype(BF16)
        kept += dot(units, place)
    upto = (iota((256, 256), 0) <= iota((256, 256), 1)).astype(F32).astype(BF16)
    place_of = dot(kept.astype(BF16), upto)
    ours = jnp.sum(jnp.where(iota((2 * CHIPS, 256), 1) < 128, kept, 0.0), axis=1, keepdims=True)
    place_of += jnp.where(iota((2 * CHIPS, 256), 1) < 128, 0.0, jnp.maximum(2 * sum(EARLY) - ours, 0.0))
    own_pos[...] = place_of * kept
    order = place_of.astype(jnp.int32) - 1
    odd = lax.rem(iota((2 * CHIPS, 256), 1), 2)
    spot = order // 2 + jnp.where(lax.rem(order + 2, 2) == odd, 0, slots)
    tabs[0 : 2 * CHIPS] = jnp.clip(jnp.where(kept > 0.5, spot, 2 * slots), 0, 2 * slots)
    taken = (own_pos[pl.ds(pa, 1), :] == (iota((256, 256), 0) + 1).astype(F32)).astype(F32).astype(BF16)
    units = iota((8, 256), 1).astype(F32).astype(BF16)
    unit = lax.dot_general(units, taken, (((1,), (1,)), ((), ())), preferred_element_type=F32).astype(jnp.int32)
    there = lax.dot_general(jnp.ones((8, 256), BF16), taken, (((1,), (1,)), ((), ())), preferred_element_type=F32).astype(jnp.int32)
    tabs[2 * CHIPS : 2 * CHIPS + 8] = jnp.clip(unit // 2, 0, 63)
    tabs[2 * CHIPS + 16 : 2 * CHIPS + 24] = unit // 128
    tabs[2 * CHIPS + 24 : 2 * CHIPS + 32] = jnp.clip(unit // 2 - 64, 0, 31)
    tabs[2 * CHIPS + 8 : 2 * CHIPS + 16] = jnp.clip(there * (1 + lax.rem(unit, 2)), 0, 2)
    to_smem = pltpu.make_async_copy(tabs, spots, s_sem)
    to_smem.start()

    pl.semaphore_wait(barrier, CHIPS + NY - 1)

    def give_x(v, carry):
        pltpu.make_async_remote_copy(
            src_ref=x_block(3, v), dst_ref=xb.at[v], send_sem=e_send, recv_sem=e_recv,
            device_id=plane(x, z, 1 - core), device_id_type=MESH,
        ).start()
        return carry

    lax.fori_loop(0, 32, give_x, 0)

    to, at = iota((256, 256), 0), iota((256, 256), 1)
    perms[0] = (at == lax.rem(to, 16) * 16 + to // 16).astype(BF16)
    perms[1] = (at == (lax.rem(to, 8) * 2 + lax.rem(to // 8, 2)) * 16 + to // 16).astype(BF16)
    perms[2] = (at == lax.rem(to, 128) // 8 * 16 + to // 128 * 8 + lax.rem(to, 8)).astype(BF16)
    frm, into = iota((SB, SB), 0), iota((SB, SB), 1)
    for h in (0, 1):
        sel[0, h] = jnp.zeros((SB, SB), BF16)
        for b in (0, 1):
            sel[1 + b, h] = ((frm - BS * b == into - BS * h) & (into // BS == h)).astype(BF16)
    sel[3, 0] = (lax.rem(frm + BS, SB) == into).astype(BF16)

    to_smem.wait()
    wait(xa, i_sem)

    for w, n in enumerate(sizes):
        if w == len(EARLY):
            wait(xb, e_recv)

        def one(i, carry):
            for k in range(2):
                r = starts[w] + i * 2 + k
                full = jnp.zeros((256, SB), F32)
                for h in (0, 1):
                    cube = xa[spots[2 * CHIPS, 2 * r + h]]
                    if w >= len(EARLY):
                        cube = jnp.where(spots[2 * CHIPS + 16, 2 * r + h] > 0, xb[spots[2 * CHIPS + 24, 2 * r + h]], cube)
                    cube = cube.reshape(256, SB)
                    full += dot(cube, sel[spots[2 * CHIPS + 8, 2 * r + h], h])
                xs[:, r] = dot(perms[0], full.astype(BF16)).astype(BF16).reshape(16, 16, SB)
            return carry

        lax.fori_loop(0, n // 2, one, 0)
        part = pl.ds(starts[w], n)
        to_chips(lambda t: xs.at[t, part], xr.at[chip, part], x_send.at[w], x_recv.at[w])

    spread = (block_of((NAO, 8), 0) == iota((NAO, 8), 1)).astype(F32)
    for g in range(3):
        this = iota((8, 8, NP // BS), 2) == (ROWS * pa + 16 * g) // BS
        rows = dot(spread, jnp.sum(jnp.where(this, mask[...].astype(F32), 0.0), axis=2))
        me[g] = lax.dot_general(rows, spread, (((1,), (1,)), ((), ())), preferred_element_type=F32).astype(BF16)
    group_row = group[...].astype(F32)
    row_group = jnp.sum(spread * group_row, axis=1, keepdims=True)
    col_group = lax.dot_general(group_row, spread, (((1,), (1,)), ((), ())), preferred_element_type=F32)
    near = jnp.abs(row_group - col_group) <= GROUP_REACH + 0.5
    vm[...] = jnp.where(near, virt[...].astype(F32), 0.0).astype(BF16)
    occ_f[...] = jnp.where(near, occ[...].astype(F32), 0.0).T
    for a in range(8):
        occ_t[a * LB : (a + 1) * LB] = occ_f[pl.ds(pl.multiple_of(a * BS + mu * LB, LB), LB), :].astype(BF16)

    def make_product(w, carry):
        for part in range(YR // SR):
            v = w * (YR // SR) + part
            tensor_chunk(v).wait()

            @pl.when(v + 1 < ROWS // SR)
            def _():
                tensor_chunk(v + 1).start()

            def one(p, carry):
                block = tb[lax.rem(v, 2), p] * me[w // 2]
                half[part * SR + p] = dot(occ_t[...], block).astype(BF16)
                return carry

            lax.fori_loop(0, SR, one, 0)
        for a in range(4):
            done = dot(half[:, a * 2 * LB : (a + 1) * 2 * LB, :].reshape(256, NAO), vm[...]).astype(BF16)
            ys[w, :, :, a * NAO : (a + 1) * NAO] = dot(perms[1], done).astype(BF16).reshape(16, 16, NAO)
        to_chips(lambda t: ys.at[w, t], yr.at[w, chip], y_send.at[w], y_recv.at[w])
        return carry

    lax.fori_loop(0, YW, make_product, 0)

    for w, n in enumerate(sizes):
        wait(xr.at[:, pl.ds(starts[w], n)], x_recv.at[w])
    left_half = iota((16, SB), 1) < BS

    def unpack(i, carry):
        rows = dot(xr[i, 0:slots].reshape(slots * 16, SB), sel[3, 0])
        xr[i, slots : 2 * slots] = rows.astype(BF16).reshape(slots, 16, SB)
        xr[i, 2 * slots] = jnp.zeros((16, SB), BF16)
        j = 2 * i + core
        for g in range(3):
            row = pl.multiple_of(granule_rows(i, core)[g], 16)
            for a in range(8):
                for b in range(4):
                    u = (g * 8 + a) * 8 + 2 * b
                    both = jnp.where(left_half, xr[i, spots[j, u]], xr[i, spots[j, u + 1]])
                    first = a % 2 * KC + a // 2 * NAO + b * SB
                    xl[pl.ds(row, 16), first : first + SB] = both
            rows = pl.ds(row, 16)
            pltpu.make_async_remote_copy(
                src_ref=xl.at[rows], dst_ref=xl.at[rows], send_sem=l_send, recv_sem=l_recv,
                device_id=plane(x, z, 1 - core), device_id_type=MESH,
            ).start()
        return carry

    lax.fori_loop(0, CHIPS, unpack, 0)
    wait(xl.at[pl.ds(0, NP // 2)], l_recv)

    def partial(w, carry):
        wait(yr.at[w], y_recv.at[w])
        for k in range(4):
            rows = yr[w, :, :, k * NAO : (k + 1) * NAO].reshape(256, NAO)
            turned = dot(perms[2], rows).astype(BF16)
            yl[:, k * NAO : (k + 1) * NAO] = turned[:WR]
            yl[:, KC + k * NAO : KC + (k + 1) * NAO] = turned[WR:]

        def tile(y2):
            columns = xl[pl.ds(pl.multiple_of(y2 * QC, QC), QC), :]
            return lax.dot_general(yl[...], columns, (((1,), (1,)), ((), ())), preferred_element_type=F32)

        for k, dy in enumerate(DY):
            y2 = lax.rem(mu + dy, NY)
            cb[w, k] = tile(y2).astype(BF16)
            pltpu.make_async_remote_copy(
                src_ref=cb.at[w, k], dst_ref=yrs.at[w, k], send_sem=c_send.at[w], recv_sem=c_recv.at[w],
                device_id=(pa, y2), device_id_type=MESH,
            ).start()
        sb[lax.rem(w, 2)] = tile(mu)

        @pl.when(w > 0)
        def _():
            sum_y(w - 1)

        return carry

    def sum_y(w):
        wait(yrs.at[w], c_recv.at[w])
        total = (sb[lax.rem(w, 2)] + yrs[w, 0].astype(F32)) + (yrs[w, 1].astype(F32) + yrs[w, 2].astype(F32))
        for k in range(YZ):

            @pl.when(lax.rem(w, YZ) == k)
            def _():
                zf[:, k * YR : (k + 1) * YR, :] = total.reshape(CHIPS, YR, QC)

        @pl.when(lax.rem(w, YZ) == YZ - 1)
        def _():
            v = w // YZ
            zb[v] = zf[...].astype(BF16)
            to_chips(lambda t: zb.at[v, t], zr.at[v, chip], z_send.at[v], z_recv.at[v])

    lax.fori_loop(0, YW, partial, 0)
    sum_y(YW - 1)

    def finish(w, carry):
        wait(zr.at[w], z_recv.at[w])
        out[pl.ds(pl.multiple_of(w * ZR, ZR), ZR), :] = jnp.sum(zr[w].astype(F32), axis=0) * (1.0 / NAO)
        return carry

    lax.fori_loop(0, ZW, finish, 0)

    wait(xb, e_send)
    wait(xl.at[pl.ds(0, NP // 2)], l_send)
    for w, n in enumerate(sizes):
        wait(xs.at[pl.ds(0, CHIPS - 1), pl.ds(0, n)], x_send.at[w])
    for w in range(YW):
        wait(yr.at[w, pl.ds(0, CHIPS - 1)], y_send.at[w])
        wait(cb.at[w], c_send.at[w])
    for w in range(ZW):
        wait(zr.at[w, pl.ds(0, CHIPS - 1)], z_send.at[w])


def packed(tier, tensor, block_mask, group_row, green_occ, green_virt):
    slots = TIERS[tier]
    waves = len(slot_waves(slots))
    vmem = pl.BlockSpec(memory_space=pltpu.VMEM)
    dma = pltpu.SemaphoreType.DMA
    return pl.pallas_call(
        functools.partial(packed_kernel, slots),
        out_shape=jax.ShapeDtypeStruct((ROWS, QC), F32),
        in_specs=[pl.BlockSpec(memory_space=pl.ANY), vmem, vmem, vmem, vmem],
        out_specs=vmem,
        scratch_shapes=[
            pltpu.VMEM((64, 16, LB, SB), BF16),
            pltpu.VMEM((32, 16, LB, SB), BF16),
            pltpu.VMEM((CHIPS, slots, 16, SB), BF16),
            pltpu.VMEM((CHIPS, 2 * slots + 1, 16, SB), BF16),
            pltpu.VMEM((NP, 2 * KC), BF16),
            pltpu.VMEM((2, SR, NAO, NAO), BF16),
            pltpu.VMEM((3, NAO, NAO), BF16),
            pltpu.VMEM((NAO, NAO), F32),
            pltpu.VMEM((SB, NAO), BF16),
            pltpu.VMEM((NAO, NAO), BF16),
            pltpu.VMEM((3, 256, 256), BF16),
            pltpu.VMEM((4, 2, SB, SB), BF16),
            pltpu.VMEM((2 * CHIPS + 32, 256), jnp.int32),
            pltpu.VMEM((2 * CHIPS, 256), F32),
            pltpu.VMEM((YR, SB, NAO), BF16),
            pltpu.VMEM((YW, CHIPS, 16, KC), BF16),
            pltpu.VMEM((YW, CHIPS, 16, KC), BF16),
            pltpu.VMEM((WR, 2 * KC), BF16),
            pltpu.VMEM((YW, NY - 1, WR, QC), BF16),
            pltpu.VMEM((2, WR, QC), F32),
            pltpu.VMEM((YW, NY - 1, WR, QC), BF16),
            pltpu.VMEM((CHIPS, ZR, QC), F32),
            pltpu.VMEM((ZW, CHIPS, ZR, QC), BF16),
            pltpu.VMEM((ZW, CHIPS, ZR, QC), BF16),
            pltpu.SMEM((2 * CHIPS + 32, 256), jnp.int32),
            dma, dma, dma, dma((waves,)), dma((waves,)), dma, dma, dma((2,)), dma((YW,)), dma((YW,)), dma((YW,)), dma((YW,)), dma((ZW,)), dma((ZW,)), dma,
        ],
        compiler_params=pltpu.CompilerParams(collective_id=1 + tier, has_side_effects=True, vmem_limit_bytes=62 * 2**20),
    )(tensor, jnp.transpose(block_mask, (1, 2, 0)), group_row, green_occ, green_virt)


def shards(tensor, block_mask, group_of_block, green_occ, green_virt):
    kept = jnp.sum(block_mask, axis=(1, 2)).reshape(NP // BS // 3, 3)
    a, b, c = kept[:, 0], kept[:, 1], kept[:, 2]
    most = 0
    for keeps, gets in ((2 * a, b), (a + b, a), (b + c, c), (2 * c, b)):
        most = jnp.maximum(most, jnp.maximum(keeps, 2 * sum(EARLY)) + gets)
    branches = [functools.partial(packed, tier) for tier in range(len(TIERS))] + [whole]
    which = jnp.max(sum((most > 2 * slots).astype(jnp.int32) for slots in TIERS))
    return lax.switch(which, branches, tensor, block_mask, group_of_block.reshape(1, 8), green_occ, green_virt)


def solution(mesh):
    placed = (P("pa", None, None), P(), P(), P(), P())
    return jax.shard_map(shards, mesh=mesh, in_specs=placed, out_specs=P("pa", "mu"), check_vma=False)
```
